32 devices in a mesh: rep: 2 (over y), frame: 16 (over z, x, core).
Axes of the slice: x: 2, y: 2, z: 4, core: 2. Of those that a mesh axis runs over, the one named last changes fastest.
Arguments:
- frames: bfloat16 [4096, 512], P(('rep', 'frame')), parts along dimension 0, may hold values from -6 to 6
- segment: int32 [4096], P(('rep', 'frame')), parts along dimension 0, may hold values from 0 to 8, as said below
- latents: bfloat16 [2048, 1024], P('frame'), may hold values from -1.5 to 1.5
- latent_queries: bfloat16 [2048, 1024], P('frame'), may hold values from -240 to 240
- w_kv: bfloat16 [512, 2048], replicated, may hold values from -0.25 to 0.25
- w_cross_out: bfloat16 [1024, 1024], replicated, may hold values from -0.1875 to 0.1875
- w_self_qkv: bfloat16 [1024, 3072], replicated
- w_self_out: bfloat16 [1024, 1024], replicated, may hold values from -0.1875 to 0.1875
Outputs:
- encoded: bfloat16 [4096, 1024], P(('rep', 'frame')), parts along dimension 0
The draws below stay inside these ranges and needn't reach their ends.
There are 2 independent parts, one for each index of `rep`. The reference program is written for one: setup_inputs(seed, part) draws one part's arguments, and reference() takes and returns one part's arrays. A program takes and returns all parts, laid end to end along the dimension named above; an argument that names none is the same for every part. Nothing has to cross between parts.
Inputs may be any that keep to these rules, and one draw needn't show every extreme that they name: `segment`: ids are constant over aligned runs of 64 frames; 0 marks silence; every id from 1 to 8 labels some frame; the share of silent frames differs between regions of the recording.
All inputs are finite; a program needn't handle non-finite values.
Results may differ from the reference program's by a relative error of at most 0.014.
The reference program's roundings to bfloat16 on the way (of `normed`, `keyval`, `cross`, `triple`, `probs` and `attended`) count: a program that leaves them out, or rounds other values in their place, can miss the bound.
Values may be sent and summed in bfloat16 or wider, within the bound.
A program may use at most 128 MiB of HBM per device.

```python
import math
import jax
import jax.numpy as jnp
from jax import lax

D = 1024
C_IN = 512
H = 16
HEAD_DIM = 64
L = 2048
NB = 8
RUN = 64
F_DEV = 128
FRAMES = 2048
N_FRAME = 16


def draw_latent_queries(key, part):
    base = jax.random.truncated_normal(jax.random.fold_in(key, 3), -4.0, 4.0, (L, D), jnp.float32) * 2.5
    return base.astype(jnp.bfloat16)


def draw_w_self_qkv(key, part):
    rest = jax.random.truncated_normal(jax.random.fold_in(key, 7), -4.0, 4.0, (D, 2 * D), jnp.float32) / math.sqrt(D)
    fresh = jax.random.truncated_normal(jax.random.fold_in(key, 5), -4.0, 4.0, (D, D), jnp.float32)
    front = fresh * (2.5 / math.sqrt(D))
    return jnp.concatenate([front, rest], axis=1).astype(jnp.bfloat16)


def draw_segment(key, part):
    runs = FRAMES // RUN
    region = jnp.arange(runs, dtype=jnp.int32) * 8 // runs
    rates = jax.random.randint(jax.random.fold_in(key, 21), (8,), 1, 10)
    silent = jax.random.randint(jax.random.fold_in(key, 22), (runs,), 0, 10) < rates[region]
    label = jax.random.randint(jax.random.fold_in(key, 23), (runs,), 1, NB + 1).astype(jnp.int32)
    label = jnp.where(silent, jnp.int32(0), label)
    order = jax.random.permutation(jax.random.fold_in(key, 24), runs)
    label = label.at[order[:NB]].set(jnp.arange(1, NB + 1, dtype=jnp.int32))
    return jnp.repeat(label, RUN, total_repeat_length=FRAMES).astype(jnp.int32)


def level_of(key, shape, split, smallest, largest):
    gain, own = 1.0, jax.random.fold_in(key, 6)
    for position, shards_of in split:
        heights = jnp.exp(jax.random.uniform(jax.random.fold_in(own, position), (shards_of,), jnp.float32, smallest / len(split), largest / len(split)))
        gain = gain * jnp.repeat(heights, shape[position] // shards_of).reshape([-1 if axis == position else 1 for axis in range(len(shape))])
    return gain


def centred(key, extent, scale, limit, split=(), held_as=jnp.bfloat16):
    result = scale * jax.random.normal(key, extent, jnp.float32)
    if split:
        result = result * level_of(key, extent, split, -0.22, 0.18)
    return jnp.clip(result, -limit, limit).astype(held_as)


def setup_inputs(seed: int = 0, part: int = 0) -> dict:
    keys = jax.random.split(jax.random.key(seed), 9)
    part_keys = jax.random.split(jax.random.fold_in(keys[8], part), 9)
    frames = centred(part_keys[0], (FRAMES, C_IN), 1.0, 6.0, ((0, 16),))
    segment = draw_segment(jax.random.fold_in(jax.random.fold_in(keys[8], part), 71), part)
    latents = centred(keys[2], (L, D), 0.25, 1.5, ((0, 16),))
    latent_queries = draw_latent_queries(jax.random.fold_in(keys[8], 71), part)
    w_kv = centred(keys[4], (C_IN, 2 * D), C_IN ** -0.5, 0.25)
    w_cross_out = centred(keys[5], (D, D), D ** -0.5, 0.1875)
    w_self_qkv = draw_w_self_qkv(jax.random.fold_in(keys[8], 71), part)
    w_self_out = centred(keys[7], (D, D), D ** -0.5, 0.1875)
    return {"frames": frames, "segment": segment, "latents": latents, "latent_queries": latent_queries, "w_kv": w_kv, "w_cross_out": w_cross_out, "w_self_qkv": w_self_qkv, "w_self_out": w_self_out}


NEG = -1e+30

def layer_norm(inputs):
    centre = inputs - lax.optimization_barrier(jnp.mean(inputs, axis=-1, keepdims=True))
    spread = lax.optimization_barrier(jnp.mean(centre * centre, axis=-1, keepdims=True))
    return centre * lax.rsqrt(spread + 1e-05)

def reference(frames, segment, latents, latent_queries, w_kv, w_cross_out, w_self_qkv, w_self_out):
    scale = 1.0 / math.sqrt(HEAD_DIM)
    normed = layer_norm(frames.astype(jnp.float32)).astype(jnp.bfloat16)
    keyval = jnp.dot(normed, w_kv, preferred_element_type=jnp.float32).astype(jnp.bfloat16)
    key_blocks = keyval[:, :D].reshape(N_FRAME, F_DEV, H, HEAD_DIM)
    value_blocks = keyval[:, D:].reshape(N_FRAME, F_DEV, H, HEAD_DIM)
    label_blocks = segment.reshape(N_FRAME, F_DEV)
    latent_full = latents.astype(jnp.float32)
    query_heads = latent_queries.reshape(L, H, HEAD_DIM).astype(jnp.float32)
    wanted = (jnp.arange(L, dtype=jnp.int32) // (L // NB) + 1).astype(jnp.int32)

    def fold_block(carry, item):
        run_max, run_total, run_acc = carry
        key_blk, value_blk, label_blk = item
        allowed = (label_blk[None, :] == wanted[:, None])[:, None, :]
        score = jnp.einsum('lhe,fhe->lhf', query_heads, key_blk.astype(jnp.float32)) * scale
        score = jnp.where(allowed, score, NEG)
        block_max = lax.optimization_barrier(jnp.max(score, axis=2))
        weights = jnp.where(allowed, jnp.exp(score - block_max[:, :, None]), 0.0)
        block_total = lax.optimization_barrier(jnp.sum(weights, axis=2))
        rounded = lax.optimization_barrier(weights.astype(jnp.bfloat16))
        block_acc = jnp.einsum('lhf,fhe->lhe', rounded.astype(jnp.float32), value_blk.astype(jnp.float32))
        new_max = jnp.maximum(run_max, block_max)
        old_factor = jnp.exp(run_max - new_max)
        new_factor = jnp.exp(block_max - new_max)
        run_total = run_total * old_factor + block_total * new_factor
        run_acc = run_acc * old_factor[:, :, None] + block_acc * new_factor[:, :, None]
        return ((new_max, run_total, run_acc), None)
    start = (jnp.full((L, H), NEG, jnp.float32), jnp.zeros((L, H), jnp.float32), jnp.zeros((L, H, HEAD_DIM), jnp.float32))
    (run_max, run_total, run_acc), _ = lax.scan(fold_block, start, (key_blocks, value_blocks, label_blocks))
    cross = (run_acc / run_total[:, :, None]).reshape(L, D).astype(jnp.bfloat16)
    mixed = latent_full + jnp.dot(cross, w_cross_out, preferred_element_type=jnp.float32)
    normed_latent = layer_norm(mixed).astype(jnp.bfloat16)
    triple = jnp.dot(normed_latent, w_self_qkv, preferred_element_type=jnp.float32).astype(jnp.bfloat16)
    self_query = triple[:, :D].reshape(L, H, HEAD_DIM).astype(jnp.float32)
    self_key = triple[:, D:2 * D].reshape(L, H, HEAD_DIM).astype(jnp.float32)
    self_value = triple[:, 2 * D:].reshape(L, H, HEAD_DIM).astype(jnp.float32)
    score = jnp.einsum('lhe,mhe->hlm', self_query, self_key) * scale
    peak = lax.optimization_barrier(jnp.max(score, axis=2, keepdims=True))
    expo = jnp.exp(score - peak)
    probs = lax.optimization_barrier((expo / lax.optimization_barrier(jnp.sum(expo, axis=2, keepdims=True))).astype(jnp.bfloat16))
    attended = jnp.einsum('hlm,mhe->lhe', probs.astype(jnp.float32), self_value)
    attended = attended.reshape(L, D).astype(jnp.bfloat16)
    return (mixed + jnp.dot(attended, w_self_out, preferred_element_type=jnp.float32)).astype(jnp.bfloat16)
```

```python
import math

import jax
import jax.numpy as jnp
from jax import lax
from jax.sharding import PartitionSpec as P

H = 16
HEAD_DIM = 64
L = 2048
NB = 8


NEG = -1e30


def layer_norm(inputs):
    centre = inputs - jnp.mean(inputs, axis=-1, keepdims=True)
    spread = jnp.mean(centre * centre, axis=-1, keepdims=True)
    return centre * lax.rsqrt(spread + 1e-05)


def shards(frames, segment, latents, latent_queries, w_kv, w_cross_out, w_self_qkv, w_self_out):
    feature_width = w_kv.shape[1] // 2
    owned_rows = latents.shape[0]
    frame_count = frames.shape[0]
    scale = 1.0 / math.sqrt(HEAD_DIM)
    block_rows = L // NB
    latent_full = latents.astype(jnp.float32)
    normed = layer_norm(frames.astype(jnp.float32)).astype(jnp.bfloat16)
    keyval = jnp.dot(normed, w_kv, preferred_element_type=jnp.float32).astype(jnp.bfloat16)
    key_heads = keyval[:, :feature_width].reshape(frame_count, H, HEAD_DIM).transpose(1, 0, 2)
    value_heads = keyval[:, feature_width:].reshape(frame_count, H, HEAD_DIM).transpose(1, 0, 2)
    total_rows = owned_rows * lax.axis_size("frame")
    piece = lax.all_gather(latent_queries, "frame", axis=0, tiled=True)
    piece_rows = piece.shape[0]
    block_ids = jnp.arange(piece_rows, dtype=jnp.int32) // block_rows + 1
    allowed = segment[None, :] == block_ids[:, None]
    query_heads = piece.reshape(piece_rows, H, HEAD_DIM).transpose(1, 0, 2)

    def one_head(item):
        query_head, key_head, value_head = item
        score = (
            jnp.einsum("re,fe->rf", query_head, key_head, preferred_element_type=jnp.float32)
            * scale
        )
        score = jnp.where(allowed, score, NEG)
        block_max = jnp.max(score, axis=1)
        weights = jnp.where(allowed, jnp.exp(score - block_max[:, None]), 0.0)
        block_total = jnp.sum(weights, axis=1)
        summed = jnp.dot(
            weights.astype(jnp.bfloat16), value_head, preferred_element_type=jnp.float32
        )
        return (block_max, block_total, summed)

    block_max, block_total, summed = lax.map(one_head, (query_heads, key_heads, value_heads))
    run_max = block_max.T
    run_total = block_total.T
    joined = summed.transpose(1, 0, 2).reshape(piece_rows, feature_width)
    run_acc = joined
    run_max, run_total, run_acc = (run_max, run_total, run_acc)
    sources = lax.axis_size("frame")
    got_acc, got_max, got_total = (
        lax.all_to_all(
            run_acc.reshape(sources, owned_rows, feature_width),
            "frame",
            split_axis=0,
            concat_axis=0,
            tiled=True,
        ),
        lax.all_to_all(
            run_max.reshape(sources, owned_rows, H),
            "frame",
            split_axis=0,
            concat_axis=0,
            tiled=True,
        ),
        lax.all_to_all(
            run_total.reshape(sources, owned_rows, H),
            "frame",
            split_axis=0,
            concat_axis=0,
            tiled=True,
        ),
    )
    global_max = jnp.max(got_max, axis=0)
    factor = jnp.exp(got_max - global_max[None])
    norms = jnp.sum(got_total * factor, axis=0)
    sums = jnp.sum(
        got_acc.reshape(sources, owned_rows, H, HEAD_DIM) * factor[:, :, :, None], axis=0
    )
    cross = (sums / norms[:, :, None]).reshape(owned_rows, feature_width)
    cross = cross.astype(jnp.bfloat16)
    mixed = latent_full + jnp.dot(cross, w_cross_out, preferred_element_type=jnp.float32)
    normed_latent = layer_norm(mixed).astype(jnp.bfloat16)
    triple = jnp.dot(normed_latent, w_self_qkv, preferred_element_type=jnp.float32).astype(
        jnp.bfloat16
    )
    self_query = triple[:, :feature_width].reshape(owned_rows, H, HEAD_DIM)
    self_key = triple[:, feature_width : 2 * feature_width]
    self_value = triple[:, 2 * feature_width :]
    every_key, every_value = (
        lax.all_gather(self_key, "frame", axis=0, tiled=True),
        lax.all_gather(self_value, "frame", axis=0, tiled=True),
    )
    every_key = every_key.reshape(total_rows, H, HEAD_DIM)
    every_value = every_value.reshape(total_rows, H, HEAD_DIM)
    score = (
        jnp.einsum("rhe,mhe->hrm", self_query, every_key, preferred_element_type=jnp.float32)
        * scale
    )
    peak = jnp.max(score, axis=2, keepdims=True)
    expo = jnp.exp(score - peak)
    probs = (expo / jnp.sum(expo, axis=2, keepdims=True)).astype(jnp.bfloat16)
    attended = jnp.einsum("hrm,mhe->rhe", probs, every_value, preferred_element_type=jnp.float32)
    attended = attended.reshape(owned_rows, feature_width).astype(jnp.bfloat16)
    return (mixed + jnp.dot(attended, w_self_out, preferred_element_type=jnp.float32)).astype(
        jnp.bfloat16
    )


def shards_small(frames, segment, latents, latent_queries, w_kv, w_cross_out, w_self_qkv, w_self_out):
    width = w_kv.shape[1] // 2
    rows = latents.shape[0]
    scale = 1.0 / math.sqrt(HEAD_DIM)
    first = lax.axis_index("frame") * rows
    own_ids = (first + jnp.arange(rows, dtype=jnp.int32)) // (L // NB) + 1
    every_frame = lax.all_gather(frames, "frame", axis=0, tiled=True)
    every_segment = lax.all_gather(segment, "frame", axis=0, tiled=True)
    normed = layer_norm(every_frame.astype(jnp.float32)).astype(jnp.bfloat16)
    keyval = jnp.dot(normed, w_kv, preferred_element_type=jnp.float32).astype(jnp.bfloat16)
    count = keyval.shape[0]
    keys = keyval[:, :width].reshape(count, H, HEAD_DIM)
    vals = keyval[:, width:].reshape(count, H, HEAD_DIM)
    queries = latent_queries.reshape(rows, H, HEAD_DIM)
    allowed = (every_segment[None, :] == own_ids[:, None])[None]
    score = jnp.einsum("rhe,fhe->hrf", queries, keys, preferred_element_type=jnp.float32) * scale
    score = jnp.where(allowed, score, NEG)
    peak = jnp.max(score, axis=2, keepdims=True)
    weights = jnp.where(allowed, jnp.exp(score - peak), 0.0)
    total = jnp.sum(weights, axis=2)
    summed = jnp.einsum(
        "hrf,fhe->hre", weights.astype(jnp.bfloat16), vals, preferred_element_type=jnp.float32
    )
    cross = (summed / total[:, :, None]).transpose(1, 0, 2).reshape(rows, width)
    cross = cross.astype(jnp.bfloat16)
    mixed = latents.astype(jnp.float32) + jnp.dot(
        cross, w_cross_out, preferred_element_type=jnp.float32
    )
    normed_latent = layer_norm(mixed).astype(jnp.bfloat16)
    every_latent = lax.all_gather(normed_latent, "frame", axis=0, tiled=True)
    self_query = jnp.dot(
        normed_latent, w_self_qkv[:, :width], preferred_element_type=jnp.float32
    ).astype(jnp.bfloat16)
    self_keyval = jnp.dot(
        every_latent, w_self_qkv[:, width:], preferred_element_type=jnp.float32
    ).astype(jnp.bfloat16)
    total_rows = every_latent.shape[0]
    self_query = self_query.reshape(rows, H, HEAD_DIM)
    self_key = self_keyval[:, :width].reshape(total_rows, H, HEAD_DIM)
    self_value = self_keyval[:, width:].reshape(total_rows, H, HEAD_DIM)
    score = (
        jnp.einsum("rhe,mhe->hrm", self_query, self_key, preferred_element_type=jnp.float32)
        * scale
    )
    peak = jnp.max(score, axis=2, keepdims=True)
    expo = jnp.exp(score - peak)
    probs = (expo / jnp.sum(expo, axis=2, keepdims=True)).astype(jnp.bfloat16)
    attended = jnp.einsum("hrm,mhe->rhe", probs, self_value, preferred_element_type=jnp.float32)
    attended = attended.reshape(rows, width).astype(jnp.bfloat16)
    return (mixed + jnp.dot(attended, w_self_out, preferred_element_type=jnp.float32)).astype(
        jnp.bfloat16
    )


def solution(mesh):
    placed = (
        P(("rep", "frame"), None),
        P(("rep", "frame")),
        P("frame", None),
        P("frame", None),
        P(),
        P(),
        P(),
        P(),
    )
    body = shards_small if mesh.shape["frame"] <= 16 else shards
    return jax.shard_map(
        body, mesh=mesh, in_specs=placed, out_specs=P(("rep", "frame"), None), check_vma=False
    )
```

```python
import math

import jax
import jax.numpy as jnp
from jax import lax
from jax.experimental import pallas as pl
from jax.experimental.pallas import tpu as pltpu
from jax.sharding import PartitionSpec as P

H = 16
HEAD_DIM = 64
L = 2048
NB = 8


NEG = -1e30


def layer_norm(inputs):
    centre = inputs - jnp.mean(inputs, axis=-1, keepdims=True)
    spread = jnp.mean(centre * centre, axis=-1, keepdims=True)
    return centre * lax.rsqrt(spread + 1e-05)


def shards(frames, segment, latents, latent_queries, w_kv, w_cross_out, w_self_qkv, w_self_out):
    feature_width = w_kv.shape[1] // 2
    owned_rows = latents.shape[0]
    frame_count = frames.shape[0]
    scale = 1.0 / math.sqrt(HEAD_DIM)
    block_rows = L // NB
    latent_full = latents.astype(jnp.float32)
    normed = layer_norm(frames.astype(jnp.float32)).astype(jnp.bfloat16)
    keyval = jnp.dot(normed, w_kv, preferred_element_type=jnp.float32).astype(jnp.bfloat16)
    key_heads = keyval[:, :feature_width].reshape(frame_count, H, HEAD_DIM).transpose(1, 0, 2)
    value_heads = keyval[:, feature_width:].reshape(frame_count, H, HEAD_DIM).transpose(1, 0, 2)
    total_rows = owned_rows * lax.axis_size("frame")
    piece = lax.all_gather(latent_queries, "frame", axis=0, tiled=True)
    piece_rows = piece.shape[0]
    block_ids = jnp.arange(piece_rows, dtype=jnp.int32) // block_rows + 1
    allowed = segment[None, :] == block_ids[:, None]
    query_heads = piece.reshape(piece_rows, H, HEAD_DIM).transpose(1, 0, 2)

    def one_head(item):
        query_head, key_head, value_head = item
        score = (
            jnp.einsum("re,fe->rf", query_head, key_head, preferred_element_type=jnp.float32)
            * scale
        )
        score = jnp.where(allowed, score, NEG)
        block_max = jnp.max(score, axis=1)
        weights = jnp.where(allowed, jnp.exp(score - block_max[:, None]), 0.0)
        block_total = jnp.sum(weights, axis=1)
        summed = jnp.dot(
            weights.astype(jnp.bfloat16), value_head, preferred_element_type=jnp.float32
        )
        return (block_max, block_total, summed)

    block_max, block_total, summed = lax.map(one_head, (query_heads, key_heads, value_heads))
    run_max = block_max.T
    run_total = block_total.T
    joined = summed.transpose(1, 0, 2).reshape(piece_rows, feature_width)
    run_acc = joined
    run_max, run_total, run_acc = (run_max, run_total, run_acc)
    sources = lax.axis_size("frame")
    got_acc, got_max, got_total = (
        lax.all_to_all(
            run_acc.reshape(sources, owned_rows, feature_width),
            "frame",
            split_axis=0,
            concat_axis=0,
            tiled=True,
        ),
        lax.all_to_all(
            run_max.reshape(sources, owned_rows, H),
            "frame",
            split_axis=0,
            concat_axis=0,
            tiled=True,
        ),
        lax.all_to_all(
            run_total.reshape(sources, owned_rows, H),
            "frame",
            split_axis=0,
            concat_axis=0,
            tiled=True,
        ),
    )
    global_max = jnp.max(got_max, axis=0)
    factor = jnp.exp(got_max - global_max[None])
    norms = jnp.sum(got_total * factor, axis=0)
    sums = jnp.sum(
        got_acc.reshape(sources, owned_rows, H, HEAD_DIM) * factor[:, :, :, None], axis=0
    )
    cross = (sums / norms[:, :, None]).reshape(owned_rows, feature_width)
    cross = cross.astype(jnp.bfloat16)
    mixed = latent_full + jnp.dot(cross, w_cross_out, preferred_element_type=jnp.float32)
    normed_latent = layer_norm(mixed).astype(jnp.bfloat16)
    triple = jnp.dot(normed_latent, w_self_qkv, preferred_element_type=jnp.float32).astype(
        jnp.bfloat16
    )
    self_query = triple[:, :feature_width].reshape(owned_rows, H, HEAD_DIM)
    self_key = triple[:, feature_width : 2 * feature_width]
    self_value = triple[:, 2 * feature_width :]
    every_key, every_value = (
        lax.all_gather(self_key, "frame", axis=0, tiled=True),
        lax.all_gather(self_value, "frame", axis=0, tiled=True),
    )
    every_key = every_key.reshape(total_rows, H, HEAD_DIM)
    every_value = every_value.reshape(total_rows, H, HEAD_DIM)
    score = (
        jnp.einsum("rhe,mhe->hrm", self_query, every_key, preferred_element_type=jnp.float32)
        * scale
    )
    peak = jnp.max(score, axis=2, keepdims=True)
    expo = jnp.exp(score - peak)
    probs = (expo / jnp.sum(expo, axis=2, keepdims=True)).astype(jnp.bfloat16)
    attended = jnp.einsum("hrm,mhe->rhe", probs, every_value, preferred_element_type=jnp.float32)
    attended = attended.reshape(owned_rows, feature_width).astype(jnp.bfloat16)
    return (mixed + jnp.dot(attended, w_self_out, preferred_element_type=jnp.float32)).astype(
        jnp.bfloat16
    )


NX = 2
NZ = 4
PAIRS = H // 2
MESH = pl.DeviceIdType.MESH


def pick(index, values):
    chosen = values[0]
    for position in range(1, len(values)):
        chosen = jnp.where(index == position, values[position], chosen)
    return chosen


class Place:
    def __init__(self):
        self.me = lax.axis_index("frame")
        self.z = self.me // 4
        self.x = lax.rem(self.me // 2, 2)
        self.core = lax.rem(self.me, 2)
        self.sibling = self.index(self.z, self.x, 1 - self.core)
        self.across = self.index(self.z, 1 - self.x, self.core)
        self.above = self.me + 4
        self.below = self.me - 4
        self.has_above = self.z < NZ - 1
        self.has_below = self.z > 0
        self.order = [
            self.z,
            pick(self.z, (1, 2, 1, 2)),
            pick(self.z, (2, 0, 3, 1)),
            pick(self.z, (3, 3, 0, 0)),
        ]

    def index(self, z, x, core):
        return z * 4 + x * 2 + core


def greet(targets):
    barrier = pltpu.get_barrier_semaphore()
    for target, there in targets:
        if there is None:
            pl.semaphore_signal(barrier, inc=1, device_id={"frame": target}, device_id_type=MESH)
        else:

            @pl.when(there)
            def _():
                pl.semaphore_signal(
                    barrier, inc=1, device_id={"frame": target}, device_id_type=MESH
                )

    return barrier


STEPS = (("z", 0), ("z", 1), ("x", 0), ("z", 2), ("x", 1), ("z", 3), ("x", 2), ("x", 3))


def push(src, dst, send, recv, target):
    return pltpu.make_async_remote_copy(
        src_ref=src,
        dst_ref=dst,
        send_sem=send,
        recv_sem=recv,
        device_id={"frame": target},
        device_id_type=MESH,
    )


def relays(place, k, slot, src, gathered, send_up, send_down, send_x, recv):
    source_z = place.order[k]
    up = jnp.logical_and(source_z <= place.z, place.has_above)
    down = jnp.logical_and(source_z >= place.z, place.has_below)
    to = gathered.at[slot]
    return [
        (push(src, to, send_up.at[k], recv.at[slot], place.above), up),
        (push(src, to, send_down.at[k], recv.at[slot], place.below), down),
        (push(src, to, send_x.at[k], recv.at[slot], place.across), None),
    ]


def start_all(copies):
    for copy, there in copies:
        if there is None:
            copy.start()
        else:
            pl.when(there)(copy.start)


def wait_sent(copies):
    for copy, there in copies:
        if there is None:
            copy.wait_send()
        else:
            pl.when(there)(copy.wait_send)


def gather_kernel(
    frames, seg, every, ids, seg8, send_up, send_down, send_x, send_core, recv, seg_send, seg_recv, local
):
    place = Place()
    me = place.me
    barrier = greet([(lax.rem(me + d, 16), None) for d in range(1, 16)])
    seg8[...] = jnp.broadcast_to(seg[...], seg8.shape)
    own = pltpu.make_async_copy(frames, every.at[me], local.at[0])
    own.start()
    own_ids = pltpu.make_async_copy(seg8, ids.at[me], local.at[1])
    own_ids.start()
    pl.semaphore_wait(barrier, 15)
    sent = []
    for kind, k in STEPS:
        x = place.x if kind == "z" else 1 - place.x
        slot = place.index(place.order[k], x, place.core)
        first = kind == "z" and k == 0
        src = frames if first else every.at[slot]
        if not first:
            push(src, every.at[slot], send_core.at[0], recv.at[slot], place.sibling).wait_recv()
        copies = []
        if kind == "z":
            copies = relays(place, k, slot, src, every, send_up, send_down, send_x, recv)
        number = k + (0 if kind == "z" else 4)
        copies.append(
            (push(src, every.at[slot], send_core.at[number], recv.at[slot], place.sibling), None)
        )
        start_all(copies)
        sent += copies
        if first:
            for d in range(1, 16):
                copy = push(
                    seg8, ids.at[me], seg_send.at[d], seg_recv.at[d], lax.rem(me + d, 16)
                )
                copy.start()
                sent.append((copy, None))
    for kind, k in STEPS:
        x = place.x if kind == "z" else 1 - place.x
        slot = place.index(place.order[k], x, 1 - place.core)
        push(
            every.at[slot], every.at[slot], send_core.at[0], recv.at[slot], place.sibling
        ).wait_recv()
    for d in range(1, 16):
        source = lax.rem(me - d + 16, 16)
        push(seg8, ids.at[source], seg_send.at[d], seg_recv.at[d], source).wait_recv()
    wait_sent(sent)
    own.wait()
    own_ids.wait()


def gather_frames(frames, segment):
    dma = pltpu.SemaphoreType.DMA
    rows, channels = frames.shape
    return pl.pallas_call(
        gather_kernel,
        out_shape=(
            jax.ShapeDtypeStruct((16, rows, channels), frames.dtype),
            jax.ShapeDtypeStruct((16, 8, rows), jnp.int32),
        ),
        in_specs=[pl.BlockSpec(memory_space=pl.ANY), pl.BlockSpec(memory_space=pltpu.VMEM)],
        out_specs=[pl.BlockSpec(memory_space=pl.ANY)] * 2,
        scratch_shapes=[
            pltpu.VMEM((8, rows), jnp.int32),
            dma((4,)),
            dma((4,)),
            dma((4,)),
            dma((8,)),
            dma((16,)),
            dma((16,)),
            dma((16,)),
            dma((2,)),
        ],
        compiler_params=pltpu.CompilerParams(
            collective_id=0, has_side_effects=True, vmem_limit_bytes=4 * 2**20
        ),
        name="gather_frames",
    )(frames, segment.reshape(1, rows))


def split_pair(pair):
    lane = lax.broadcasted_iota(jnp.int32, pair.shape, 1)
    zero = jnp.zeros_like(pair)
    return jnp.concatenate(
        [jnp.where(lane < HEAD_DIM, pair, zero), jnp.where(lane < HEAD_DIM, zero, pair)], axis=0
    )


def clear(peak, total, acc):
    peak[...] = jnp.full(peak.shape, -jnp.inf, jnp.float32)
    total[...] = jnp.zeros(total.shape, jnp.float32)
    acc[...] = jnp.zeros(acc.shape, jnp.float32)


def attend(p, query, key, value, peak, total, acc, keep=None):
    score = lax.dot_general(
        query, key, (((1,), (1,)), ((), ())), preferred_element_type=jnp.float32
    )
    if keep is not None:
        column = lax.broadcasted_iota(jnp.int32, score.shape, 1)
        score = jnp.where(column < keep, score, -jnp.inf)
    before = peak[p]
    now = jnp.maximum(before, jnp.max(score, axis=1, keepdims=True))
    half = now.shape[1]
    left = jnp.exp(score[:, :half] - now)
    right = jnp.exp(score[:, half:] - now)
    fade = jnp.exp(before - now)
    peak[p] = now
    total[p] = total[p] * fade + (left + right)
    weights = jnp.concatenate([left.astype(jnp.bfloat16), right.astype(jnp.bfloat16)], axis=1)
    acc[p] = acc[p] * fade + jnp.dot(weights, value, preferred_element_type=jnp.float32)


def join_pair(p, total, acc):
    rows = acc.shape[1] // 2
    result = acc[p] / jnp.sum(total[p], axis=1, keepdims=True)
    lane = lax.broadcasted_iota(jnp.int32, (rows, acc.shape[2]), 1)
    return jnp.where(lane < HEAD_DIM, result[:rows], result[rows:]).astype(jnp.bfloat16)


def pair_columns(p):
    return pl.ds(pl.multiple_of(p * 128, 128), 128)


def cross_kernel(
    ids, every, queries, latents, w_kv, w_out, mixed, normed, block, keyval, query, peak, total,
    acc, cross, chosen, sems
):
    wanted = lax.axis_index("frame") // 2 + 1
    width = queries.shape[1]
    scale = 1.0 / math.sqrt(HEAD_DIM)

    def look(r, count):
        chosen[count] = r
        return count + jnp.where(ids[r // 2, 0, lax.rem(r, 2) * 64] == wanted, 1, 0)

    count = lax.fori_loop(0, 32, look, jnp.int32(0))
    block[...] = jnp.zeros_like(block)

    def fetch(group, j):
        run = chosen[group * 4 + j]
        return pltpu.make_async_copy(
            every.at[run // 2, pl.ds(pl.multiple_of(lax.rem(run, 2) * 64, 64), 64)],
            block.at[pl.ds(j * 64, 64)],
            sems.at[j],
        )

    def fetch_all(group):
        for j in range(4):

            @pl.when(group * 4 + j < count)
            def _():
                fetch(group, j).start()

    fetch_all(0)
    for p in range(PAIRS):
        query[p] = split_pair(queries[:, p * 128 : p * 128 + 128] * scale)
    clear(peak, total, acc)

    @pl.loop(0, (count + 3) // 4)
    def _(group):
        for j in range(4):

            @pl.when(group * 4 + j < count)
            def _():
                fetch(group, j).wait()

        ready = layer_norm(block[...].astype(jnp.float32)).astype(jnp.bfloat16)

        @pl.loop(0, 4)
        def _(j):
            columns = pl.ds(pl.multiple_of(j * 512, 512), 512)
            keyval[:, columns] = jnp.dot(
                ready, w_kv[:, columns], preferred_element_type=jnp.float32
            ).astype(jnp.bfloat16)

        fetch_all(group + 1)
        keep = (count - group * 4) * 64

        @pl.loop(0, PAIRS, unroll=2)
        def _(p):
            attend(
                p, query[p], keyval[:, pair_columns(p)], keyval[:, pair_columns(p + PAIRS)],
                peak, total, acc, keep,
            )

    for p in range(PAIRS):
        cross[:, p * 128 : p * 128 + 128] = join_pair(p, total, acc)
    whole = latents[...].astype(jnp.float32) + jnp.dot(
        cross[...], w_out[...], preferred_element_type=jnp.float32
    )
    mixed[...] = whole
    normed[...] = layer_norm(whole).astype(jnp.bfloat16)


def cross_attend(ids, every, queries, latents, w_kv, w_out):
    rows, width = latents.shape
    vmem = pl.BlockSpec(memory_space=pltpu.VMEM)
    return pl.pallas_call(
        cross_kernel,
        out_shape=(
            jax.ShapeDtypeStruct((rows, width), jnp.float32),
            jax.ShapeDtypeStruct((rows, width), jnp.bfloat16),
        ),
        in_specs=[
            pl.BlockSpec(memory_space=pltpu.SMEM),
            pl.BlockSpec(memory_space=pl.ANY),
            vmem,
            vmem,
            vmem,
            vmem,
        ],
        out_specs=[vmem, vmem],
        scratch_shapes=[
            pltpu.VMEM((256, every.shape[2]), jnp.bfloat16),
            pltpu.VMEM((256, 2 * width), jnp.bfloat16),
            pltpu.VMEM((PAIRS, 2 * rows, 128), jnp.bfloat16),
            pltpu.VMEM((PAIRS, 2 * rows, 128), jnp.float32),
            pltpu.VMEM((PAIRS, 2 * rows, 128), jnp.float32),
            pltpu.VMEM((PAIRS, 2 * rows, 128), jnp.float32),
            pltpu.VMEM((rows, width), jnp.bfloat16),
            pltpu.SMEM((64,), jnp.int32),
            pltpu.SemaphoreType.DMA((4,)),
        ],
        compiler_params=pltpu.CompilerParams(vmem_limit_bytes=24 * 2**20),
        name="cross_attend",
    )(ids, every, queries, latents, w_kv, w_out)


def self_kernel(
    normed, mixed, w_qkv, w_out, out, gathered, keyval, weights, weights_out, query, peak, total,
    acc, joined, send_up, send_down, send_x, send_core, recv, recv_core, local
):
    place = Place()
    me = place.me
    rows, width = normed.shape
    scale = 1.0 / math.sqrt(HEAD_DIM)
    barrier = greet(
        [
            (place.sibling, None),
            (place.across, None),
            (place.above, place.has_above),
            (place.below, place.has_below),
        ]
    )
    load = pltpu.make_async_copy(w_qkv, weights, local.at[0])
    load.start()
    load_out = pltpu.make_async_copy(w_out, weights_out, local.at[1])
    load_out.start()
    pl.semaphore_wait(
        barrier,
        2 + jnp.where(place.has_above, 1, 0) + jnp.where(place.has_below, 1, 0),
    )
    clear(peak, total, acc)
    sent = []

    def take(step):
        kind, k = STEPS[step]
        x = place.x if kind == "z" else 1 - place.x
        slot = place.index(place.order[k], x, place.core)
        chip = place.order[k] * 2 + x
        src = normed if step == 0 else gathered.at[slot]
        if step > 0:
            push(src, gathered.at[slot], send_x.at[0], recv.at[slot], place.across).wait_recv()
        if kind == "z":
            copies = relays(place, k, slot, src, gathered, send_up, send_down, send_x, recv)
            start_all(copies)
            sent.extend(copies)
        if step == 0:
            load.wait()

            @pl.loop(0, PAIRS // 2)
            def _(j):
                columns = pl.ds(pl.multiple_of(j * 256, 256), 256)
                part = jnp.dot(normed[...], weights[:, columns], preferred_element_type=jnp.float32)
                part = part.astype(jnp.bfloat16) * scale
                query[2 * j] = split_pair(part[:, :128])
                query[2 * j + 1] = split_pair(part[:, 128:])

        @pl.loop(0, 4)
        def _(j):
            columns = pl.ds(pl.multiple_of(j * 512, 512), 512)
            wide = pl.ds(pl.multiple_of(width + j * 512, 512), 512)
            keyval[chip, place.core, :, columns] = jnp.dot(
                src[...], weights[:, wide], preferred_element_type=jnp.float32
            ).astype(jnp.bfloat16)

        ours = keyval.at[chip, place.core]
        copy = push(ours, ours, send_core.at[step], recv_core.at[step], place.sibling)
        copy.start()
        sent.append((copy, None))
        return chip

    def use(step, chip):
        theirs = keyval.at[chip, 1 - place.core]
        push(theirs, theirs, send_core.at[step], recv_core.at[step], place.sibling).wait_recv()

        @pl.loop(0, PAIRS, unroll=2)
        def _(p):
            key = keyval[chip, :, :, pair_columns(p)].reshape(2 * rows, 128)
            value = keyval[chip, :, :, pair_columns(p + PAIRS)].reshape(2 * rows, 128)
            attend(p, query[p], key, value, peak, total, acc)

    chip = take(0)
    for step in range(1, len(STEPS)):
        later = take(step)
        use(step - 1, chip)
        chip = later
    use(len(STEPS) - 1, chip)
    for p in range(PAIRS):
        joined[:, p * 128 : p * 128 + 128] = join_pair(p, total, acc)
    load_out.wait()
    out[...] = (
        mixed[...] + jnp.dot(joined[...], weights_out[...], preferred_element_type=jnp.float32)
    ).astype(jnp.bfloat16)
    wait_sent(sent)


def self_attend(normed, mixed, w_qkv, w_out):
    rows, width = normed.shape
    dma = pltpu.SemaphoreType.DMA
    vmem = pl.BlockSpec(memory_space=pltpu.VMEM)
    anywhere = pl.BlockSpec(memory_space=pl.ANY)
    return pl.pallas_call(
        self_kernel,
        out_shape=jax.ShapeDtypeStruct((rows, width), jnp.bfloat16),
        in_specs=[vmem, vmem, anywhere, anywhere],
        out_specs=vmem,
        scratch_shapes=[
            pltpu.VMEM((16, rows, width), jnp.bfloat16),
            pltpu.VMEM((8, 2, rows, 2 * width), jnp.bfloat16),
            pltpu.VMEM(w_qkv.shape, jnp.bfloat16),
            pltpu.VMEM(w_out.shape, jnp.bfloat16),
            pltpu.VMEM((PAIRS, 2 * rows, 128), jnp.bfloat16),
            pltpu.VMEM((PAIRS, 2 * rows, 128), jnp.float32),
            pltpu.VMEM((PAIRS, 2 * rows, 128), jnp.float32),
            pltpu.VMEM((PAIRS, 2 * rows, 128), jnp.float32),
            pltpu.VMEM((rows, width), jnp.bfloat16),
            dma((4,)),
            dma((4,)),
            dma((4,)),
            dma((8,)),
            dma((16,)),
            dma((8,)),
            dma((2,)),
        ],
        compiler_params=pltpu.CompilerParams(
            collective_id=1, has_side_effects=True, vmem_limit_bytes=40 * 2**20
        ),
        name="self_attend",
    )(normed, mixed, w_qkv, w_out)


def shards_small(frames, segment, latents, latent_queries, w_kv, w_cross_out, w_self_qkv, w_self_out):
    every, ids = gather_frames(frames, segment)
    mixed, normed = cross_attend(ids, every, latent_queries, latents, w_kv, w_cross_out)
    return self_attend(normed, mixed, w_self_qkv, w_self_out)


def solution(mesh):
    placed = (
        P(("rep", "frame"), None),
        P(("rep", "frame")),
        P("frame", None),
        P("frame", None),
        P(),
        P(),
        P(),
        P(),
    )
    body = shards_small if mesh.shape["frame"] == 2 * NX * NZ else shards
    return jax.shard_map(
        body, mesh=mesh, in_specs=placed, out_specs=P(("rep", "frame"), None), check_vma=False
    )
```

```python
import math

import jax
import jax.numpy as jnp
from jax import lax
from jax.experimental import pallas as pl
from jax.experimental.pallas import tpu as pltpu
from jax.sharding import PartitionSpec as P

H = 16
HEAD_DIM = 64
L = 2048
NB = 8


NEG = -1e30


def layer_norm(inputs):
    centre = inputs - jnp.mean(inputs, axis=-1, keepdims=True)
    spread = jnp.mean(centre * centre, axis=-1, keepdims=True)
    return centre * lax.rsqrt(spread + 1e-05)


def shards(frames, segment, latents, latent_queries, w_kv, w_cross_out, w_self_qkv, w_self_out):
    feature_width = w_kv.shape[1] // 2
    owned_rows = latents.shape[0]
    frame_count = frames.shape[0]
    scale = 1.0 / math.sqrt(HEAD_DIM)
    block_rows = L // NB
    latent_full = latents.astype(jnp.float32)
    normed = layer_norm(frames.astype(jnp.float32)).astype(jnp.bfloat16)
    keyval = jnp.dot(normed, w_kv, preferred_element_type=jnp.float32).astype(jnp.bfloat16)
    key_heads = keyval[:, :feature_width].reshape(frame_count, H, HEAD_DIM).transpose(1, 0, 2)
    value_heads = keyval[:, feature_width:].reshape(frame_count, H, HEAD_DIM).transpose(1, 0, 2)
    total_rows = owned_rows * lax.axis_size("frame")
    piece = lax.all_gather(latent_queries, "frame", axis=0, tiled=True)
    piece_rows = piece.shape[0]
    block_ids = jnp.arange(piece_rows, dtype=jnp.int32) // block_rows + 1
    allowed = segment[None, :] == block_ids[:, None]
    query_heads = piece.reshape(piece_rows, H, HEAD_DIM).transpose(1, 0, 2)

    def one_head(item):
        query_head, key_head, value_head = item
        score = (
            jnp.einsum("re,fe->rf", query_head, key_head, preferred_element_type=jnp.float32)
            * scale
        )
        score = jnp.where(allowed, score, NEG)
        block_max = jnp.max(score, axis=1)
        weights = jnp.where(allowed, jnp.exp(score - block_max[:, None]), 0.0)
        block_total = jnp.sum(weights, axis=1)
        summed = jnp.dot(
            weights.astype(jnp.bfloat16), value_head, preferred_element_type=jnp.float32
        )
        return (block_max, block_total, summed)

    block_max, block_total, summed = lax.map(one_head, (query_heads, key_heads, value_heads))
    run_max = block_max.T
    run_total = block_total.T
    joined = summed.transpose(1, 0, 2).reshape(piece_rows, feature_width)
    run_acc = joined
    run_max, run_total, run_acc = (run_max, run_total, run_acc)
    sources = lax.axis_size("frame")
    got_acc, got_max, got_total = (
        lax.all_to_all(
            run_acc.reshape(sources, owned_rows, feature_width),
            "frame",
            split_axis=0,
            concat_axis=0,
            tiled=True,
        ),
        lax.all_to_all(
            run_max.reshape(sources, owned_rows, H),
            "frame",
            split_axis=0,
            concat_axis=0,
            tiled=True,
        ),
        lax.all_to_all(
            run_total.reshape(sources, owned_rows, H),
            "frame",
            split_axis=0,
            concat_axis=0,
            tiled=True,
        ),
    )
    global_max = jnp.max(got_max, axis=0)
    factor = jnp.exp(got_max - global_max[None])
    norms = jnp.sum(got_total * factor, axis=0)
    sums = jnp.sum(
        got_acc.reshape(sources, owned_rows, H, HEAD_DIM) * factor[:, :, :, None], axis=0
    )
    cross = (sums / norms[:, :, None]).reshape(owned_rows, feature_width)
    cross = cross.astype(jnp.bfloat16)
    mixed = latent_full + jnp.dot(cross, w_cross_out, preferred_element_type=jnp.float32)
    normed_latent = layer_norm(mixed).astype(jnp.bfloat16)
    triple = jnp.dot(normed_latent, w_self_qkv, preferred_element_type=jnp.float32).astype(
        jnp.bfloat16
    )
    self_query = triple[:, :feature_width].reshape(owned_rows, H, HEAD_DIM)
    self_key = triple[:, feature_width : 2 * feature_width]
    self_value = triple[:, 2 * feature_width :]
    every_key, every_value = (
        lax.all_gather(self_key, "frame", axis=0, tiled=True),
        lax.all_gather(self_value, "frame", axis=0, tiled=True),
    )
    every_key = every_key.reshape(total_rows, H, HEAD_DIM)
    every_value = every_value.reshape(total_rows, H, HEAD_DIM)
    score = (
        jnp.einsum("rhe,mhe->hrm", self_query, every_key, preferred_element_type=jnp.float32)
        * scale
    )
    peak = jnp.max(score, axis=2, keepdims=True)
    expo = jnp.exp(score - peak)
    probs = (expo / jnp.sum(expo, axis=2, keepdims=True)).astype(jnp.bfloat16)
    attended = jnp.einsum("hrm,mhe->rhe", probs, every_value, preferred_element_type=jnp.float32)
    attended = attended.reshape(owned_rows, feature_width).astype(jnp.bfloat16)
    return (mixed + jnp.dot(attended, w_self_out, preferred_element_type=jnp.float32)).astype(
        jnp.bfloat16
    )


NX = 2
NZ = 4
PAIRS = H // 2
MESH = pl.DeviceIdType.MESH


def pick(index, values):
    chosen = values[0]
    for position in range(1, len(values)):
        chosen = jnp.where(index == position, values[position], chosen)
    return chosen


class Place:
    def __init__(self):
        self.me = lax.axis_index("frame")
        self.z = self.me // 4
        self.x = lax.rem(self.me // 2, 2)
        self.core = lax.rem(self.me, 2)
        self.sibling = self.index(self.z, self.x, 1 - self.core)
        self.across = self.index(self.z, 1 - self.x, self.core)
        self.above = self.me + 4
        self.below = self.me - 4
        self.has_above = self.z < NZ - 1
        self.has_below = self.z > 0
        self.order = [
            self.z,
            pick(self.z, (1, 2, 1, 2)),
            pick(self.z, (2, 0, 3, 1)),
            pick(self.z, (3, 3, 0, 0)),
        ]

    def index(self, z, x, core):
        return z * 4 + x * 2 + core


def greet(targets):
    barrier = pltpu.get_barrier_semaphore()
    for target, there in targets:
        if there is None:
            pl.semaphore_signal(barrier, inc=1, device_id={"frame": target}, device_id_type=MESH)
        else:

            @pl.when(there)
            def _():
                pl.semaphore_signal(
                    barrier, inc=1, device_id={"frame": target}, device_id_type=MESH
                )

    return barrier


STEPS = (("z", 0), ("z", 1), ("x", 0), ("z", 2), ("x", 1), ("z", 3), ("x", 2), ("x", 3))


def push(src, dst, send, recv, target):
    return pltpu.make_async_remote_copy(
        src_ref=src,
        dst_ref=dst,
        send_sem=send,
        recv_sem=recv,
        device_id={"frame": target},
        device_id_type=MESH,
    )


def relays(place, k, slot, src, gathered, send_up, send_down, send_x, recv):
    source_z = place.order[k]
    up = jnp.logical_and(source_z <= place.z, place.has_above)
    down = jnp.logical_and(source_z >= place.z, place.has_below)
    to = gathered.at[slot]
    return [
        (push(src, to, send_up.at[k], recv.at[slot], place.above), up),
        (push(src, to, send_down.at[k], recv.at[slot], place.below), down),
        (push(src, to, send_x.at[k], recv.at[slot], place.across), None),
    ]


def start_all(copies):
    for copy, there in copies:
        if there is None:
            copy.start()
        else:
            pl.when(there)(copy.start)


def wait_sent(copies):
    for copy, there in copies:
        if there is None:
            copy.wait_send()
        else:
            pl.when(there)(copy.wait_send)


def gather_kernel(
    frames, seg, every, ids, seg1, seg8, send_up, send_down, send_x, send_core, recv, seg_send,
    seg_recv, local
):
    place = Place()
    me = place.me
    barrier = greet([(lax.rem(me + d, 16), None) for d in range(1, 16)])
    load = pltpu.make_async_copy(seg, seg1, local.at[2])
    load.start()
    load.wait()
    seg8[...] = jnp.broadcast_to(seg1[...], seg8.shape)
    own = pltpu.make_async_copy(frames, every.at[me], local.at[0])
    own.start()
    own_ids = pltpu.make_async_copy(seg8, ids.at[me], local.at[1])
    own_ids.start()
    pl.semaphore_wait(barrier, 15)
    sent = []
    for kind, k in STEPS:
        x = place.x if kind == "z" else 1 - place.x
        slot = place.index(place.order[k], x, place.core)
        first = kind == "z" and k == 0
        src = frames if first else every.at[slot]
        if not first:
            push(src, every.at[slot], send_core.at[0], recv.at[slot], place.sibling).wait_recv()
        copies = []
        if kind == "z":
            copies = relays(place, k, slot, src, every, send_up, send_down, send_x, recv)
        number = k + (0 if kind == "z" else 4)
        copies.append(
            (push(src, every.at[slot], send_core.at[number], recv.at[slot], place.sibling), None)
        )
        start_all(copies)
        sent += copies
        if first:
            for d in range(1, 16):
                copy = push(
                    seg8, ids.at[me], seg_send.at[d], seg_recv.at[d], lax.rem(me + d, 16)
                )
                copy.start()
                sent.append((copy, None))
    for kind, k in STEPS:
        x = place.x if kind == "z" else 1 - place.x
        slot = place.index(place.order[k], x, 1 - place.core)
        push(
            every.at[slot], every.at[slot], send_core.at[0], recv.at[slot], place.sibling
        ).wait_recv()
    for d in range(1, 16):
        source = lax.rem(me - d + 16, 16)
        push(seg8, ids.at[source], seg_send.at[d], seg_recv.at[d], source).wait_recv()
    wait_sent(sent)
    own.wait()
    own_ids.wait()


def gather_frames(frames, segment):
    dma = pltpu.SemaphoreType.DMA
    rows, channels = frames.shape
    return pl.pallas_call(
        gather_kernel,
        out_shape=(
            jax.ShapeDtypeStruct((16, rows, channels), frames.dtype),
            jax.ShapeDtypeStruct((16, 8, rows), jnp.int32),
        ),
        in_specs=[pl.BlockSpec(memory_space=pl.ANY)] * 2,
        out_specs=[pl.BlockSpec(memory_space=pl.ANY)] * 2,
        scratch_shapes=[
            pltpu.VMEM((1, rows), jnp.int32),
            pltpu.VMEM((8, rows), jnp.int32),
            dma((4,)),
            dma((4,)),
            dma((4,)),
            dma((8,)),
            dma((16,)),
            dma((16,)),
            dma((16,)),
            dma((3,)),
        ],
        compiler_params=pltpu.CompilerParams(
            collective_id=0, has_side_effects=True, vmem_limit_bytes=62 * 2**20
        ),
        name="gather_frames",
    )(frames, segment.reshape(1, rows))


def split_pair(pair):
    lane = lax.broadcasted_iota(jnp.int32, pair.shape, 1)
    zero = jnp.zeros_like(pair)
    return jnp.concatenate(
        [jnp.where(lane < HEAD_DIM, pair, zero), jnp.where(lane < HEAD_DIM, zero, pair)], axis=0
    )


def clear(peak, total, acc):
    peak[...] = jnp.full(peak.shape, -jnp.inf, jnp.float32)
    total[...] = jnp.zeros(total.shape, jnp.float32)
    acc[...] = jnp.zeros(acc.shape, jnp.float32)


def attend(pairs, queries, keys, values, peak, total, acc, keep=None):
    scores = [
        lax.dot_general(query, key, (((1,), (1,)), ((), ())), preferred_element_type=jnp.float32)
        for query, key in zip(queries, keys)
    ]
    if keep is not None:
        column = lax.broadcasted_iota(jnp.int32, scores[0].shape, 1)
        scores = [jnp.where(column < keep, score, -jnp.inf) for score in scores]
    before = [peak[p] for p in pairs]
    old_total = [total[p] for p in pairs]
    old_acc = [acc[p] for p in pairs]
    now = [
        jnp.maximum(b, jnp.max(score, axis=1, keepdims=True)) for b, score in zip(before, scores)
    ]
    half = now[0].shape[1]
    left = [jnp.exp(score[:, :half] - n) for score, n in zip(scores, now)]
    right = [jnp.exp(score[:, half:] - n) for score, n in zip(scores, now)]
    fade = [jnp.exp(b - n) for b, n in zip(before, now)]
    weights = [
        jnp.concatenate([a.astype(jnp.bfloat16), b.astype(jnp.bfloat16)], axis=1)
        for a, b in zip(left, right)
    ]
    added = [
        jnp.dot(w, value, preferred_element_type=jnp.float32) for w, value in zip(weights, values)
    ]
    new_total = [t * f + (a + b) for t, f, a, b in zip(old_total, fade, left, right)]
    new_acc = [o * f + a for o, f, a in zip(old_acc, fade, added)]
    for position, p in enumerate(pairs):
        peak[p] = now[position]
        total[p] = new_total[position]
        acc[p] = new_acc[position]


def join_pair(p, total, acc):
    rows = acc.shape[1] // 2
    result = acc[p] / jnp.sum(total[p], axis=1, keepdims=True)
    lane = lax.broadcasted_iota(jnp.int32, (rows, acc.shape[2]), 1)
    return jnp.where(lane < HEAD_DIM, result[:rows], result[rows:]).astype(jnp.bfloat16)


def pair_columns(p):
    return pl.ds(pl.multiple_of(p * 128, 128), 128)


def cross_kernel(
    ids, every, queries_all, latents_all, w_kv_all, w_out_all, mixed, normed, block, keyval, query,
    peak, total, acc, cross, queries, latents, w_kv, w_out, chosen, sems, local
):
    loads = [
        pltpu.make_async_copy(src, dst, local.at[n])
        for n, (src, dst) in enumerate(
            [(queries_all, queries), (w_kv_all, w_kv), (w_out_all, w_out), (latents_all, latents)]
        )
    ]
    for load in loads[:2]:
        load.start()
    wanted = lax.axis_index("frame") // 2 + 1
    width = queries.shape[1]
    scale = 1.0 / math.sqrt(HEAD_DIM)

    def look(r, count):
        chosen[count] = r
        return count + jnp.where(ids[r // 2, 0, lax.rem(r, 2) * 64] == wanted, 1, 0)

    count = lax.fori_loop(0, 32, look, jnp.int32(0))
    block[...] = jnp.zeros_like(block)

    def fetch(group, j):
        run = chosen[group * 4 + j]
        return pltpu.make_async_copy(
            every.at[run // 2, pl.ds(pl.multiple_of(lax.rem(run, 2) * 64, 64), 64)],
            block.at[pl.ds(j * 64, 64)],
            sems.at[j],
        )

    def fetch_all(group):
        for j in range(4):

            @pl.when(group * 4 + j < count)
            def _():
                fetch(group, j).start()

    fetch_all(0)
    for load in loads[2:]:
        load.start()
    loads[0].wait()
    for p in range(PAIRS):
        query[p] = split_pair(queries[:, p * 128 : p * 128 + 128] * scale)
    clear(peak, total, acc)
    loads[1].wait()

    @pl.loop(0, (count + 3) // 4)
    def _(group):
        for j in range(4):

            @pl.when(group * 4 + j < count)
            def _():
                fetch(group, j).wait()

        ready = layer_norm(block[...].astype(jnp.float32)).astype(jnp.bfloat16)

        @pl.loop(0, 4)
        def _(j):
            columns = pl.ds(pl.multiple_of(j * 512, 512), 512)
            keyval[:, columns] = jnp.dot(
                ready, w_kv[:, columns], preferred_element_type=jnp.float32
            ).astype(jnp.bfloat16)

        fetch_all(group + 1)
        keep = (count - group * 4) * 64

        @pl.loop(0, PAIRS // 4)
        def _(group):
            pairs = [group * 4 + i for i in range(4)]
            attend(
                pairs,
                [query[p] for p in pairs],
                [keyval[:, pair_columns(p)] for p in pairs],
                [keyval[:, pair_columns(p + PAIRS)] for p in pairs],
                peak,
                total,
                acc,
                keep,
            )

    for p in range(PAIRS):
        cross[:, p * 128 : p * 128 + 128] = join_pair(p, total, acc)
    loads[2].wait()
    loads[3].wait()
    whole = latents[...].astype(jnp.float32) + jnp.dot(
        cross[...], w_out[...], preferred_element_type=jnp.float32
    )
    mixed[...] = whole
    normed[...] = layer_norm(whole).astype(jnp.bfloat16)


def cross_attend(ids, every, queries, latents, w_kv, w_out):
    rows, width = latents.shape
    vmem = pl.BlockSpec(memory_space=pltpu.VMEM)
    return pl.pallas_call(
        cross_kernel,
        out_shape=(
            jax.ShapeDtypeStruct((rows, width), jnp.float32),
            jax.ShapeDtypeStruct((rows, width), jnp.bfloat16),
        ),
        in_specs=[
            pl.BlockSpec(memory_space=pltpu.SMEM),
            *[pl.BlockSpec(memory_space=pl.ANY)] * 5,
        ],
        out_specs=[vmem, vmem],
        scratch_shapes=[
            pltpu.VMEM((256, every.shape[2]), jnp.bfloat16),
            pltpu.VMEM((256, 2 * width), jnp.bfloat16),
            pltpu.VMEM((PAIRS, 2 * rows, 128), jnp.bfloat16),
            pltpu.VMEM((PAIRS, 2 * rows, 128), jnp.float32),
            pltpu.VMEM((PAIRS, 2 * rows, 128), jnp.float32),
            pltpu.VMEM((PAIRS, 2 * rows, 128), jnp.float32),
            pltpu.VMEM((rows, width), jnp.bfloat16),
            pltpu.VMEM(queries.shape, jnp.bfloat16),
            pltpu.VMEM(latents.shape, jnp.bfloat16),
            pltpu.VMEM(w_kv.shape, jnp.bfloat16),
            pltpu.VMEM(w_out.shape, jnp.bfloat16),
            pltpu.SMEM((64,), jnp.int32),
            pltpu.SemaphoreType.DMA((4,)),
            pltpu.SemaphoreType.DMA((4,)),
        ],
        compiler_params=pltpu.CompilerParams(vmem_limit_bytes=61 * 2**20),
        name="cross_attend",
    )(ids, every, queries, latents, w_kv, w_out)


def self_kernel(
    normed, mixed, w_qkv, w_out, out, gathered, keyval, weights, weights_out, query, peak, total,
    acc, joined, send_up, send_down, send_x, send_core, recv, recv_core, local
):
    place = Place()
    me = place.me
    rows, width = normed.shape
    scale = 1.0 / math.sqrt(HEAD_DIM)
    barrier = greet(
        [
            (place.sibling, None),
            (place.across, None),
            (place.above, place.has_above),
            (place.below, place.has_below),
        ]
    )
    load = pltpu.make_async_copy(w_qkv, weights, local.at[0])
    load.start()
    load_out = pltpu.make_async_copy(w_out, weights_out, local.at[1])
    load_out.start()
    pl.semaphore_wait(
        barrier,
        2 + jnp.where(place.has_above, 1, 0) + jnp.where(place.has_below, 1, 0),
    )
    clear(peak, total, acc)
    sent = []

    def take(step):
        kind, k = STEPS[step]
        x = place.x if kind == "z" else 1 - place.x
        slot = place.index(place.order[k], x, place.core)
        chip = place.order[k] * 2 + x
        src = normed if step == 0 else gathered.at[slot]
        if step > 0:
            push(src, gathered.at[slot], send_x.at[0], recv.at[slot], place.across).wait_recv()
        if kind == "z":
            copies = relays(place, k, slot, src, gathered, send_up, send_down, send_x, recv)
            start_all(copies)
            sent.extend(copies)
        if step == 0:
            load.wait()

            @pl.loop(0, PAIRS // 2)
            def _(j):
                columns = pl.ds(pl.multiple_of(j * 256, 256), 256)
                part = jnp.dot(normed[...], weights[:, columns], preferred_element_type=jnp.float32)
                part = part.astype(jnp.bfloat16) * scale
                query[2 * j] = split_pair(part[:, :128])
                query[2 * j + 1] = split_pair(part[:, 128:])

        @pl.loop(0, 4)
        def _(j):
            columns = pl.ds(pl.multiple_of(j * 512, 512), 512)
            wide = pl.ds(pl.multiple_of(width + j * 512, 512), 512)
            keyval[chip, place.core, :, columns] = jnp.dot(
                src[...], weights[:, wide], preferred_element_type=jnp.float32
            ).astype(jnp.bfloat16)

        ours = keyval.at[chip, place.core]
        copy = push(ours, ours, send_core.at[step], recv_core.at[step], place.sibling)
        copy.start()
        sent.append((copy, None))
        return chip

    def use(step, chip):
        theirs = keyval.at[chip, 1 - place.core]
        push(theirs, theirs, send_core.at[step], recv_core.at[step], place.sibling).wait_recv()

        @pl.loop(0, PAIRS // 4)
        def _(group):
            pairs = [group * 4 + i for i in range(4)]
            attend(
                pairs,
                [query[p] for p in pairs],
                [keyval[chip, :, :, pair_columns(p)].reshape(2 * rows, 128) for p in pairs],
                [
                    keyval[chip, :, :, pair_columns(p + PAIRS)].reshape(2 * rows, 128)
                    for p in pairs
                ],
                peak,
                total,
                acc,
            )

    chip = take(0)
    for step in range(1, len(STEPS)):
        later = take(step)
        use(step - 1, chip)
        chip = later
    use(len(STEPS) - 1, chip)
    for p in range(PAIRS):
        joined[:, p * 128 : p * 128 + 128] = join_pair(p, total, acc)
    load_out.wait()
    out[...] = (
        mixed[...] + jnp.dot(joined[...], weights_out[...], preferred_element_type=jnp.float32)
    ).astype(jnp.bfloat16)
    wait_sent(sent)


def self_attend(normed, mixed, w_qkv, w_out):
    rows, width = normed.shape
    dma = pltpu.SemaphoreType.DMA
    vmem = pl.BlockSpec(memory_space=pltpu.VMEM)
    anywhere = pl.BlockSpec(memory_space=pl.ANY)
    return pl.pallas_call(
        self_kernel,
        out_shape=jax.ShapeDtypeStruct((rows, width), jnp.bfloat16),
        in_specs=[vmem, vmem, anywhere, anywhere],
        out_specs=vmem,
        scratch_shapes=[
            pltpu.VMEM((16, rows, width), jnp.bfloat16),
            pltpu.VMEM((8, 2, rows, 2 * width), jnp.bfloat16),
            pltpu.VMEM(w_qkv.shape, jnp.bfloat16),
            pltpu.VMEM(w_out.shape, jnp.bfloat16),
            pltpu.VMEM((PAIRS, 2 * rows, 128), jnp.bfloat16),
            pltpu.VMEM((PAIRS, 2 * rows, 128), jnp.float32),
            pltpu.VMEM((PAIRS, 2 * rows, 128), jnp.float32),
            pltpu.VMEM((PAIRS, 2 * rows, 128), jnp.float32),
            pltpu.VMEM((rows, width), jnp.bfloat16),
            dma((4,)),
            dma((4,)),
            dma((4,)),
            dma((8,)),
            dma((16,)),
            dma((8,)),
            dma((2,)),
        ],
        compiler_params=pltpu.CompilerParams(
            collective_id=1, has_side_effects=True, vmem_limit_bytes=60 * 2**20
        ),
        name="self_attend",
    )(normed, mixed, w_qkv, w_out)


def shards_small(frames, segment, latents, latent_queries, w_kv, w_cross_out, w_self_qkv, w_self_out):
    every, ids = gather_frames(frames, segment)
    mixed, normed = cross_attend(ids, every, latent_queries, latents, w_kv, w_cross_out)
    return self_attend(normed, mixed, w_self_qkv, w_self_out)


def solution(mesh):
    placed = (
        P(("rep", "frame"), None),
        P(("rep", "frame")),
        P("frame", None),
        P("frame", None),
        P(),
        P(),
        P(),
        P(),
    )
    body = shards_small if mesh.shape["frame"] == 2 * NX * NZ else shards
    return jax.shard_map(
        body, mesh=mesh, in_specs=placed, out_specs=P(("rep", "frame"), None), check_vma=False
    )
```

```python
import math

import jax
import jax.numpy as jnp
from jax import lax
from jax.experimental import pallas as pl
from jax.experimental.pallas import tpu as pltpu
from jax.sharding import PartitionSpec as P

H = 16
HEAD_DIM = 64
L = 2048
NB = 8


NEG = -1e30


def layer_norm(inputs):
    centre = inputs - jnp.mean(inputs, axis=-1, keepdims=True)
    spread = jnp.mean(centre * centre, axis=-1, keepdims=True)
    return centre * lax.rsqrt(spread + 1e-05)


def shards(frames, segment, latents, latent_queries, w_kv, w_cross_out, w_self_qkv, w_self_out):
    feature_width = w_kv.shape[1] // 2
    owned_rows = latents.shape[0]
    frame_count = frames.shape[0]
    scale = 1.0 / math.sqrt(HEAD_DIM)
    block_rows = L // NB
    latent_full = latents.astype(jnp.float32)
    normed = layer_norm(frames.astype(jnp.float32)).astype(jnp.bfloat16)
    keyval = jnp.dot(normed, w_kv, preferred_element_type=jnp.float32).astype(jnp.bfloat16)
    key_heads = keyval[:, :feature_width].reshape(frame_count, H, HEAD_DIM).transpose(1, 0, 2)
    value_heads = keyval[:, feature_width:].reshape(frame_count, H, HEAD_DIM).transpose(1, 0, 2)
    total_rows = owned_rows * lax.axis_size("frame")
    piece = lax.all_gather(latent_queries, "frame", axis=0, tiled=True)
    piece_rows = piece.shape[0]
    block_ids = jnp.arange(piece_rows, dtype=jnp.int32) // block_rows + 1
    allowed = segment[None, :] == block_ids[:, None]
    query_heads = piece.reshape(piece_rows, H, HEAD_DIM).transpose(1, 0, 2)

    def one_head(item):
        query_head, key_head, value_head = item
        score = (
            jnp.einsum("re,fe->rf", query_head, key_head, preferred_element_type=jnp.float32)
            * scale
        )
        score = jnp.where(allowed, score, NEG)
        block_max = jnp.max(score, axis=1)
        weights = jnp.where(allowed, jnp.exp(score - block_max[:, None]), 0.0)
        block_total = jnp.sum(weights, axis=1)
        summed = jnp.dot(
            weights.astype(jnp.bfloat16), value_head, preferred_element_type=jnp.float32
        )
        return (block_max, block_total, summed)

    block_max, block_total, summed = lax.map(one_head, (query_heads, key_heads, value_heads))
    run_max = block_max.T
    run_total = block_total.T
    joined = summed.transpose(1, 0, 2).reshape(piece_rows, feature_width)
    run_acc = joined
    run_max, run_total, run_acc = (run_max, run_total, run_acc)
    sources = lax.axis_size("frame")
    got_acc, got_max, got_total = (
        lax.all_to_all(
            run_acc.reshape(sources, owned_rows, feature_width),
            "frame",
            split_axis=0,
            concat_axis=0,
            tiled=True,
        ),
        lax.all_to_all(
            run_max.reshape(sources, owned_rows, H),
            "frame",
            split_axis=0,
            concat_axis=0,
            tiled=True,
        ),
        lax.all_to_all(
            run_total.reshape(sources, owned_rows, H),
            "frame",
            split_axis=0,
            concat_axis=0,
            tiled=True,
        ),
    )
    global_max = jnp.max(got_max, axis=0)
    factor = jnp.exp(got_max - global_max[None])
    norms = jnp.sum(got_total * factor, axis=0)
    sums = jnp.sum(
        got_acc.reshape(sources, owned_rows, H, HEAD_DIM) * factor[:, :, :, None], axis=0
    )
    cross = (sums / norms[:, :, None]).reshape(owned_rows, feature_width)
    cross = cross.astype(jnp.bfloat16)
    mixed = latent_full + jnp.dot(cross, w_cross_out, preferred_element_type=jnp.float32)
    normed_latent = layer_norm(mixed).astype(jnp.bfloat16)
    triple = jnp.dot(normed_latent, w_self_qkv, preferred_element_type=jnp.float32).astype(
        jnp.bfloat16
    )
    self_query = triple[:, :feature_width].reshape(owned_rows, H, HEAD_DIM)
    self_key = triple[:, feature_width : 2 * feature_width]
    self_value = triple[:, 2 * feature_width :]
    every_key, every_value = (
        lax.all_gather(self_key, "frame", axis=0, tiled=True),
        lax.all_gather(self_value, "frame", axis=0, tiled=True),
    )
    every_key = every_key.reshape(total_rows, H, HEAD_DIM)
    every_value = every_value.reshape(total_rows, H, HEAD_DIM)
    score = (
        jnp.einsum("rhe,mhe->hrm", self_query, every_key, preferred_element_type=jnp.float32)
        * scale
    )
    peak = jnp.max(score, axis=2, keepdims=True)
    expo = jnp.exp(score - peak)
    probs = (expo / jnp.sum(expo, axis=2, keepdims=True)).astype(jnp.bfloat16)
    attended = jnp.einsum("hrm,mhe->rhe", probs, every_value, preferred_element_type=jnp.float32)
    attended = attended.reshape(owned_rows, feature_width).astype(jnp.bfloat16)
    return (mixed + jnp.dot(attended, w_self_out, preferred_element_type=jnp.float32)).astype(
        jnp.bfloat16
    )


PARTS = 2
NX = 2
NZ = 4
PAIRS = H // 2
MESH = pl.DeviceIdType.MESH


def pick(index, values):
    chosen = values[0]
    for position in range(1, len(values)):
        chosen = jnp.where(index == position, values[position], chosen)
    return chosen


class Place:
    def __init__(self):
        self.me = lax.axis_index("frame")
        self.z = self.me // 4
        self.x = lax.rem(self.me // 2, 2)
        self.core = lax.rem(self.me, 2)
        self.sibling = self.index(self.z, self.x, 1 - self.core)
        self.across = self.index(self.z, 1 - self.x, self.core)
        self.above = self.me + 4
        self.below = self.me - 4
        self.has_above = self.z < NZ - 1
        self.has_below = self.z > 0
        self.order = [
            self.z,
            pick(self.z, (1, 2, 1, 2)),
            pick(self.z, (2, 0, 3, 1)),
            pick(self.z, (3, 3, 0, 0)),
        ]

    def index(self, z, x, core):
        return z * 4 + x * 2 + core


def greet(targets):
    barrier = pltpu.get_barrier_semaphore()
    for target, there in targets:
        if there is None:
            pl.semaphore_signal(barrier, inc=1, device_id={"frame": target}, device_id_type=MESH)
        else:

            @pl.when(there)
            def _():
                pl.semaphore_signal(
                    barrier, inc=1, device_id={"frame": target}, device_id_type=MESH
                )

    return barrier


STEPS = (("z", 0), ("z", 1), ("x", 0), ("z", 2), ("x", 1), ("z", 3), ("x", 2), ("x", 3))


def push(src, dst, send, recv, target):
    return pltpu.make_async_remote_copy(
        src_ref=src,
        dst_ref=dst,
        send_sem=send,
        recv_sem=recv,
        device_id={"frame": target},
        device_id_type=MESH,
    )


def piece(ref, part):
    rows = ref.shape[0] // PARTS
    return ref.at[pl.ds(part * rows, rows)]


def relays(place, k, part, src, to, send_up, send_down, send_x, arrived):
    source_z = place.order[k]
    up = jnp.logical_and(source_z <= place.z, place.has_above)
    down = jnp.logical_and(source_z >= place.z, place.has_below)
    number = k * PARTS + part
    return [
        (push(src, to, send_x.at[number], arrived, place.across), None),
        (push(src, to, send_up.at[number], arrived, place.above), up),
        (push(src, to, send_down.at[number], arrived, place.below), down),
    ]


def start_all(copies):
    for copy, there in copies:
        if there is None:
            copy.start()
        else:
            pl.when(there)(copy.start)


def wait_sent(copies):
    for copy, there in copies:
        if there is None:
            copy.wait_send()
        else:
            pl.when(there)(copy.wait_send)


def gather_kernel(
    frames, seg, every, ids, seg1, seg8, send_up, send_down, send_x, send_core, recv, seg_send,
    seg_recv, local
):
    place = Place()
    me = place.me
    barrier = greet([(lax.rem(me + d, 16), None) for d in range(1, 16)])
    load = pltpu.make_async_copy(seg, seg1, local.at[2])
    load.start()
    load.wait()
    seg8[...] = jnp.broadcast_to(seg1[...], seg8.shape)
    own = pltpu.make_async_copy(frames, every.at[me], local.at[0])
    own.start()
    own_ids = pltpu.make_async_copy(seg8, ids.at[me], local.at[1])
    own_ids.start()
    pl.semaphore_wait(barrier, 15)
    sent = []
    for kind, k in [("z", 0), ("z", 1), ("z", 2), ("z", 3), ("x", 0), ("x", 1), ("x", 2), ("x", 3)]:
        x = place.x if kind == "z" else 1 - place.x
        slot = place.index(place.order[k], x, place.core)
        first = kind == "z" and k == 0
        for part in range(PARTS):
            to = piece(every.at[slot], part)
            src = piece(frames, part) if first else to
            arrived = recv.at[slot * PARTS + part]
            if not first:
                push(src, to, send_core.at[0], arrived, place.sibling).wait_recv()
            copies = []
            if kind == "z":
                copies = relays(place, k, part, src, to, send_up, send_down, send_x, arrived)
            number = (k + (0 if kind == "z" else 4)) * PARTS + part
            copies.append((push(src, to, send_core.at[number], arrived, place.sibling), None))
            start_all(copies)
            sent += copies
        if first:
            for d in range(1, 16):
                copy = push(
                    seg8, ids.at[me], seg_send.at[d], seg_recv.at[d], lax.rem(me + d, 16)
                )
                copy.start()
                sent.append((copy, None))
    for kind, k in STEPS:
        x = place.x if kind == "z" else 1 - place.x
        slot = place.index(place.order[k], x, 1 - place.core)
        for part in range(PARTS):
            to = piece(every.at[slot], part)
            push(
                to, to, send_core.at[0], recv.at[slot * PARTS + part], place.sibling
            ).wait_recv()
    for d in range(1, 16):
        source = lax.rem(me - d + 16, 16)
        push(seg8, ids.at[source], seg_send.at[d], seg_recv.at[d], source).wait_recv()
    wait_sent(sent)
    own.wait()
    own_ids.wait()


def gather_frames(frames, segment):
    dma = pltpu.SemaphoreType.DMA
    rows, channels = frames.shape
    return pl.pallas_call(
        gather_kernel,
        out_shape=(
            jax.ShapeDtypeStruct((16, rows, channels), frames.dtype),
            jax.ShapeDtypeStruct((16, 8, rows), jnp.int32),
        ),
        in_specs=[pl.BlockSpec(memory_space=pl.ANY)] * 2,
        out_specs=[pl.BlockSpec(memory_space=pl.ANY)] * 2,
        scratch_shapes=[
            pltpu.VMEM((1, rows), jnp.int32),
            pltpu.VMEM((8, rows), jnp.int32),
            dma((4 * PARTS,)),
            dma((4 * PARTS,)),
            dma((4 * PARTS,)),
            dma((8 * PARTS,)),
            dma((16 * PARTS,)),
            dma((16,)),
            dma((16,)),
            dma((3,)),
        ],
        compiler_params=pltpu.CompilerParams(
            collective_id=0, has_side_effects=True, vmem_limit_bytes=62 * 2**20
        ),
        name="gather_frames",
    )(frames, segment.reshape(1, rows))


def split_pair(pair):
    lane = lax.broadcasted_iota(jnp.int32, pair.shape, 1)
    zero = jnp.zeros_like(pair)
    return jnp.concatenate(
        [jnp.where(lane < HEAD_DIM, pair, zero), jnp.where(lane < HEAD_DIM, zero, pair)], axis=0
    )


def clear(peak, total, acc):
    peak[...] = jnp.full(peak.shape, -jnp.inf, jnp.float32)
    total[...] = jnp.zeros(total.shape, jnp.float32)
    acc[...] = jnp.zeros(acc.shape, jnp.float32)


def attend(pairs, queries, keys, values, peak, total, acc, keep=None):
    scores = [
        lax.dot_general(query, key, (((1,), (1,)), ((), ())), preferred_element_type=jnp.float32)
        for query, key in zip(queries, keys)
    ]
    if keep is not None:
        column = lax.broadcasted_iota(jnp.int32, scores[0].shape, 1)
        scores = [jnp.where(column < keep, score, -jnp.inf) for score in scores]
    before = [peak[p] for p in pairs]
    old_total = [total[p] for p in pairs]
    old_acc = [acc[p] for p in pairs]
    now = [
        jnp.maximum(b, jnp.max(score, axis=1, keepdims=True)) for b, score in zip(before, scores)
    ]
    half = now[0].shape[1]
    left = [jnp.exp(score[:, :half] - n) for score, n in zip(scores, now)]
    right = [jnp.exp(score[:, half:] - n) for score, n in zip(scores, now)]
    fade = [jnp.exp(b - n) for b, n in zip(before, now)]
    weights = [
        jnp.concatenate([a.astype(jnp.bfloat16), b.astype(jnp.bfloat16)], axis=1)
        for a, b in zip(left, right)
    ]
    added = [
        jnp.dot(w, value, preferred_element_type=jnp.float32) for w, value in zip(weights, values)
    ]
    new_total = [t * f + (a + b) for t, f, a, b in zip(old_total, fade, left, right)]
    new_acc = [o * f + a for o, f, a in zip(old_acc, fade, added)]
    for position, p in enumerate(pairs):
        peak[p] = now[position]
        total[p] = new_total[position]
        acc[p] = new_acc[position]


def join_pair(p, total, acc):
    rows = acc.shape[1] // 2
    result = acc[p] / jnp.sum(total[p], axis=1, keepdims=True)
    lane = lax.broadcasted_iota(jnp.int32, (rows, acc.shape[2]), 1)
    return jnp.where(lane < HEAD_DIM, result[:rows], result[rows:]).astype(jnp.bfloat16)


def pair_columns(p):
    return pl.ds(pl.multiple_of(p * 128, 128), 128)


def cross_kernel(
    ids, every, queries_all, latents_all, w_kv_all, w_out_all, mixed, normed, block, keyval, query,
    peak, total, acc, cross, queries, latents, w_kv, w_out, chosen, sems, local
):
    loads = [
        pltpu.make_async_copy(src, dst, local.at[n])
        for n, (src, dst) in enumerate(
            [(queries_all, queries), (w_kv_all, w_kv), (w_out_all, w_out), (latents_all, latents)]
        )
    ]
    for load in loads[:2]:
        load.start()
    wanted = lax.axis_index("frame") // 2 + 1
    width = queries.shape[1]
    scale = 1.0 / math.sqrt(HEAD_DIM)

    def look(r, count):
        chosen[count] = r
        return count + jnp.where(ids[r // 2, 0, lax.rem(r, 2) * 64] == wanted, 1, 0)

    count = lax.fori_loop(0, 32, look, jnp.int32(0))
    block[...] = jnp.zeros_like(block)

    def fetch(group, j):
        run = chosen[group * 4 + j]
        return pltpu.make_async_copy(
            every.at[run // 2, pl.ds(pl.multiple_of(lax.rem(run, 2) * 64, 64), 64)],
            block.at[pl.ds(j * 64, 64)],
            sems.at[j],
        )

    def fetch_all(group):
        for j in range(4):

            @pl.when(group * 4 + j < count)
            def _():
                fetch(group, j).start()

    fetch_all(0)
    for load in loads[2:]:
        load.start()
    loads[0].wait()
    for p in range(PAIRS):
        query[p] = split_pair(queries[:, p * 128 : p * 128 + 128] * scale)
    clear(peak, total, acc)
    loads[1].wait()

    @pl.loop(0, (count + 3) // 4)
    def _(group):
        for j in range(4):

            @pl.when(group * 4 + j < count)
            def _():
                fetch(group, j).wait()

        ready = layer_norm(block[...].astype(jnp.float32)).astype(jnp.bfloat16)

        @pl.loop(0, 4)
        def _(j):
            columns = pl.ds(pl.multiple_of(j * 512, 512), 512)
            keyval[:, columns] = jnp.dot(
                ready, w_kv[:, columns], preferred_element_type=jnp.float32
            ).astype(jnp.bfloat16)

        fetch_all(group + 1)
        keep = (count - group * 4) * 64

        @pl.loop(0, PAIRS // 4)
        def _(group):
            pairs = [group * 4 + i for i in range(4)]
            attend(
                pairs,
                [query[p] for p in pairs],
                [keyval[:, pair_columns(p)] for p in pairs],
                [keyval[:, pair_columns(p + PAIRS)] for p in pairs],
                peak,
                total,
                acc,
                keep,
            )

    for p in range(PAIRS):
        cross[:, p * 128 : p * 128 + 128] = join_pair(p, total, acc)
    loads[2].wait()
    loads[3].wait()
    whole = latents[...].astype(jnp.float32) + jnp.dot(
        cross[...], w_out[...], preferred_element_type=jnp.float32
    )
    mixed[...] = whole
    normed[...] = layer_norm(whole).astype(jnp.bfloat16)


def cross_attend(ids, every, queries, latents, w_kv, w_out):
    rows, width = latents.shape
    vmem = pl.BlockSpec(memory_space=pltpu.VMEM)
    return pl.pallas_call(
        cross_kernel,
        out_shape=(
            jax.ShapeDtypeStruct((rows, width), jnp.float32),
            jax.ShapeDtypeStruct((rows, width), jnp.bfloat16),
        ),
        in_specs=[
            pl.BlockSpec(memory_space=pltpu.SMEM),
            *[pl.BlockSpec(memory_space=pl.ANY)] * 5,
        ],
        out_specs=[vmem, vmem],
        scratch_shapes=[
            pltpu.VMEM((256, every.shape[2]), jnp.bfloat16),
            pltpu.VMEM((256, 2 * width), jnp.bfloat16),
            pltpu.VMEM((PAIRS, 2 * rows, 128), jnp.bfloat16),
            pltpu.VMEM((PAIRS, 2 * rows, 128), jnp.float32),
            pltpu.VMEM((PAIRS, 2 * rows, 128), jnp.float32),
            pltpu.VMEM((PAIRS, 2 * rows, 128), jnp.float32),
            pltpu.VMEM((rows, width), jnp.bfloat16),
            pltpu.VMEM(queries.shape, jnp.bfloat16),
            pltpu.VMEM(latents.shape, jnp.bfloat16),
            pltpu.VMEM(w_kv.shape, jnp.bfloat16),
            pltpu.VMEM(w_out.shape, jnp.bfloat16),
            pltpu.SMEM((64,), jnp.int32),
            pltpu.SemaphoreType.DMA((4,)),
            pltpu.SemaphoreType.DMA((4,)),
        ],
        compiler_params=pltpu.CompilerParams(vmem_limit_bytes=61 * 2**20),
        name="cross_attend",
    )(ids, every, queries, latents, w_kv, w_out)


def self_kernel(
    normed, mixed, w_qkv, w_out, out, gathered, keyval, weights, weights_out, query, peak, total,
    acc, joined, send_up, send_down, send_x, send_core, recv, recv_core, local
):
    place = Place()
    me = place.me
    rows, width = normed.shape
    scale = 1.0 / math.sqrt(HEAD_DIM)
    barrier = greet(
        [
            (place.sibling, None),
            (place.across, None),
            (place.above, place.has_above),
            (place.below, place.has_below),
        ]
    )
    load = pltpu.make_async_copy(w_qkv, weights, local.at[0])
    load.start()
    load_out = pltpu.make_async_copy(w_out, weights_out, local.at[1])
    load_out.start()
    pl.semaphore_wait(
        barrier,
        2 + jnp.where(place.has_above, 1, 0) + jnp.where(place.has_below, 1, 0),
    )
    clear(peak, total, acc)
    sent = []

    def hand_on(k, when=None):
        slot = place.index(place.order[k], place.x, place.core)
        pieces = []
        for part in range(PARTS):
            to = piece(gathered.at[slot], part)
            src = piece(normed, part) if k == 0 else to
            arrived = recv.at[slot * PARTS + part]
            copies = relays(place, k, part, src, to, send_up, send_down, send_x, arrived)
            landing = push(src, to, send_x.at[0], arrived, place.across) if k > 0 else None
            pieces.append((landing, copies))

        def go():
            for landing, copies in pieces:
                if landing is not None:
                    landing.wait_recv()
                start_all(copies)

        if when is None:
            go()
        else:
            pl.when(when)(go)
        return [copy for _, copies in pieces for copy in copies]

    def take(step):
        kind, k = STEPS[step]
        x = place.x if kind == "z" else 1 - place.x
        slot = place.index(place.order[k], x, place.core)
        chip = place.order[k] * 2 + x
        src = normed if step == 0 else gathered.at[slot]
        if kind == "x":
            for part in range(PARTS):
                to = piece(gathered.at[slot], part)
                arrived = recv.at[slot * PARTS + part]
                push(to, to, send_x.at[0], arrived, place.across).wait_recv()
        if step == 0:
            load.wait()

            @pl.loop(0, PAIRS // 2)
            def _(j):
                columns = pl.ds(pl.multiple_of(j * 256, 256), 256)
                part = jnp.dot(normed[...], weights[:, columns], preferred_element_type=jnp.float32)
                part = part.astype(jnp.bfloat16) * scale
                query[2 * j] = split_pair(part[:, :128])
                query[2 * j + 1] = split_pair(part[:, 128:])

        @pl.loop(0, 4)
        def _(j):
            columns = pl.ds(pl.multiple_of(j * 512, 512), 512)
            wide = pl.ds(pl.multiple_of(width + j * 512, 512), 512)
            keyval[chip, place.core, :, columns] = jnp.dot(
                src[...], weights[:, wide], preferred_element_type=jnp.float32
            ).astype(jnp.bfloat16)

        ours = keyval.at[chip, place.core]
        copy = push(ours, ours, send_core.at[step], recv_core.at[step], place.sibling)
        copy.start()
        sent.append((copy, None))
        return chip

    def use(step, chip):
        theirs = keyval.at[chip, 1 - place.core]
        push(theirs, theirs, send_core.at[step], recv_core.at[step], place.sibling).wait_recv()

        @pl.loop(0, PAIRS // 4)
        def _(group):
            pairs = [group * 4 + i for i in range(4)]
            attend(
                pairs,
                [query[p] for p in pairs],
                [keyval[chip, :, :, pair_columns(p)].reshape(2 * rows, 128) for p in pairs],
                [
                    keyval[chip, :, :, pair_columns(p + PAIRS)].reshape(2 * rows, 128)
                    for p in pairs
                ],
                peak,
                total,
                acc,
            )

    inner = jnp.logical_and(place.has_above, place.has_below)
    outer = jnp.logical_not(inner)
    sent += hand_on(0)
    chip = take(0)
    for step in range(1, len(STEPS)):
        if step == 1:
            sent += hand_on(1)
            sent += hand_on(2, inner)
        elif step == 3:
            hand_on(2, outer)
            sent += hand_on(3, inner)
        elif step == 5:
            hand_on(3, outer)
        later = take(step)
        use(step - 1, chip)
        chip = later
    use(len(STEPS) - 1, chip)
    for p in range(PAIRS):
        joined[:, p * 128 : p * 128 + 128] = join_pair(p, total, acc)
    load_out.wait()
    out[...] = (
        mixed[...] + jnp.dot(joined[...], weights_out[...], preferred_element_type=jnp.float32)
    ).astype(jnp.bfloat16)
    wait_sent(sent)


def self_attend(normed, mixed, w_qkv, w_out):
    rows, width = normed.shape
    dma = pltpu.SemaphoreType.DMA
    vmem = pl.BlockSpec(memory_space=pltpu.VMEM)
    anywhere = pl.BlockSpec(memory_space=pl.ANY)
    return pl.pallas_call(
        self_kernel,
        out_shape=jax.ShapeDtypeStruct((rows, width), jnp.bfloat16),
        in_specs=[vmem, vmem, anywhere, anywhere],
        out_specs=vmem,
        scratch_shapes=[
            pltpu.VMEM((16, rows, width), jnp.bfloat16),
            pltpu.VMEM((8, 2, rows, 2 * width), jnp.bfloat16),
            pltpu.VMEM(w_qkv.shape, jnp.bfloat16),
            pltpu.VMEM(w_out.shape, jnp.bfloat16),
            pltpu.VMEM((PAIRS, 2 * rows, 128), jnp.bfloat16),
            pltpu.VMEM((PAIRS, 2 * rows, 128), jnp.float32),
            pltpu.VMEM((PAIRS, 2 * rows, 128), jnp.float32),
            pltpu.VMEM((PAIRS, 2 * rows, 128), jnp.float32),
            pltpu.VMEM((rows, width), jnp.bfloat16),
            dma((4 * PARTS,)),
            dma((4 * PARTS,)),
            dma((4 * PARTS,)),
            dma((8,)),
            dma((16 * PARTS,)),
            dma((8,)),
            dma((2,)),
        ],
        compiler_params=pltpu.CompilerParams(
            collective_id=1, has_side_effects=True, vmem_limit_bytes=60 * 2**20
        ),
        name="self_attend",
    )(normed, mixed, w_qkv, w_out)


def shards_small(frames, segment, latents, latent_queries, w_kv, w_cross_out, w_self_qkv, w_self_out):
    every, ids = gather_frames(frames, segment)
    mixed, normed = cross_attend(ids, every, latent_queries, latents, w_kv, w_cross_out)
    return self_attend(normed, mixed, w_self_qkv, w_self_out)


def solution(mesh):
    placed = (
        P(("rep", "frame"), None),
        P(("rep", "frame")),
        P("frame", None),
        P("frame", None),
        P(),
        P(),
        P(),
        P(),
    )
    body = shards_small if mesh.shape["frame"] == 2 * NX * NZ else shards
    return jax.shard_map(
        body, mesh=mesh, in_specs=placed, out_specs=P(("rep", "frame"), None), check_vma=False
    )
```

```python
import math

import jax
import jax.numpy as jnp
from jax import lax
from jax.experimental import pallas as pl
from jax.experimental.pallas import tpu as pltpu
from jax.sharding import PartitionSpec as P

H = 16
HEAD_DIM = 64
L = 2048
NB = 8


NEG = -1e30


def layer_norm(inputs):
    centre = inputs - jnp.mean(inputs, axis=-1, keepdims=True)
    spread = jnp.mean(centre * centre, axis=-1, keepdims=True)
    return centre * lax.rsqrt(spread + 1e-05)


def shards(frames, segment, latents, latent_queries, w_kv, w_cross_out, w_self_qkv, w_self_out):
    feature_width = w_kv.shape[1] // 2
    owned_rows = latents.shape[0]
    frame_count = frames.shape[0]
    scale = 1.0 / math.sqrt(HEAD_DIM)
    block_rows = L // NB
    latent_full = latents.astype(jnp.float32)
    normed = layer_norm(frames.astype(jnp.float32)).astype(jnp.bfloat16)
    keyval = jnp.dot(normed, w_kv, preferred_element_type=jnp.float32).astype(jnp.bfloat16)
    key_heads = keyval[:, :feature_width].reshape(frame_count, H, HEAD_DIM).transpose(1, 0, 2)
    value_heads = keyval[:, feature_width:].reshape(frame_count, H, HEAD_DIM).transpose(1, 0, 2)
    total_rows = owned_rows * lax.axis_size("frame")
    piece = lax.all_gather(latent_queries, "frame", axis=0, tiled=True)
    piece_rows = piece.shape[0]
    block_ids = jnp.arange(piece_rows, dtype=jnp.int32) // block_rows + 1
    allowed = segment[None, :] == block_ids[:, None]
    query_heads = piece.reshape(piece_rows, H, HEAD_DIM).transpose(1, 0, 2)

    def one_head(item):
        query_head, key_head, value_head = item
        score = (
            jnp.einsum("re,fe->rf", query_head, key_head, preferred_element_type=jnp.float32)
            * scale
        )
        score = jnp.where(allowed, score, NEG)
        block_max = jnp.max(score, axis=1)
        weights = jnp.where(allowed, jnp.exp(score - block_max[:, None]), 0.0)
        block_total = jnp.sum(weights, axis=1)
        summed = jnp.dot(
            weights.astype(jnp.bfloat16), value_head, preferred_element_type=jnp.float32
        )
        return (block_max, block_total, summed)

    block_max, block_total, summed = lax.map(one_head, (query_heads, key_heads, value_heads))
    run_max = block_max.T
    run_total = block_total.T
    joined = summed.transpose(1, 0, 2).reshape(piece_rows, feature_width)
    run_acc = joined
    run_max, run_total, run_acc = (run_max, run_total, run_acc)
    sources = lax.axis_size("frame")
    got_acc, got_max, got_total = (
        lax.all_to_all(
            run_acc.reshape(sources, owned_rows, feature_width),
            "frame",
            split_axis=0,
            concat_axis=0,
            tiled=True,
        ),
        lax.all_to_all(
            run_max.reshape(sources, owned_rows, H),
            "frame",
            split_axis=0,
            concat_axis=0,
            tiled=True,
        ),
        lax.all_to_all(
            run_total.reshape(sources, owned_rows, H),
            "frame",
            split_axis=0,
            concat_axis=0,
            tiled=True,
        ),
    )
    global_max = jnp.max(got_max, axis=0)
    factor = jnp.exp(got_max - global_max[None])
    norms = jnp.sum(got_total * factor, axis=0)
    sums = jnp.sum(
        got_acc.reshape(sources, owned_rows, H, HEAD_DIM) * factor[:, :, :, None], axis=0
    )
    cross = (sums / norms[:, :, None]).reshape(owned_rows, feature_width)
    cross = cross.astype(jnp.bfloat16)
    mixed = latent_full + jnp.dot(cross, w_cross_out, preferred_element_type=jnp.float32)
    normed_latent = layer_norm(mixed).astype(jnp.bfloat16)
    triple = jnp.dot(normed_latent, w_self_qkv, preferred_element_type=jnp.float32).astype(
        jnp.bfloat16
    )
    self_query = triple[:, :feature_width].reshape(owned_rows, H, HEAD_DIM)
    self_key = triple[:, feature_width : 2 * feature_width]
    self_value = triple[:, 2 * feature_width :]
    every_key, every_value = (
        lax.all_gather(self_key, "frame", axis=0, tiled=True),
        lax.all_gather(self_value, "frame", axis=0, tiled=True),
    )
    every_key = every_key.reshape(total_rows, H, HEAD_DIM)
    every_value = every_value.reshape(total_rows, H, HEAD_DIM)
    score = (
        jnp.einsum("rhe,mhe->hrm", self_query, every_key, preferred_element_type=jnp.float32)
        * scale
    )
    peak = jnp.max(score, axis=2, keepdims=True)
    expo = jnp.exp(score - peak)
    probs = (expo / jnp.sum(expo, axis=2, keepdims=True)).astype(jnp.bfloat16)
    attended = jnp.einsum("hrm,mhe->rhe", probs, every_value, preferred_element_type=jnp.float32)
    attended = attended.reshape(owned_rows, feature_width).astype(jnp.bfloat16)
    return (mixed + jnp.dot(attended, w_self_out, preferred_element_type=jnp.float32)).astype(
        jnp.bfloat16
    )


PARTS = 2
NX = 2
NZ = 4
PAIRS = H // 2
MESH = pl.DeviceIdType.MESH


def pick(index, values):
    chosen = values[0]
    for position in range(1, len(values)):
        chosen = jnp.where(index == position, values[position], chosen)
    return chosen


class Place:
    def __init__(self):
        self.me = lax.axis_index("frame")
        self.z = self.me // 4
        self.x = lax.rem(self.me // 2, 2)
        self.core = lax.rem(self.me, 2)
        self.sibling = self.index(self.z, self.x, 1 - self.core)
        self.across = self.index(self.z, 1 - self.x, self.core)
        self.above = self.me + 4
        self.below = self.me - 4
        self.has_above = self.z < NZ - 1
        self.has_below = self.z > 0
        self.inner = jnp.logical_and(self.has_above, self.has_below)
        self.outer = jnp.logical_not(self.inner)
        self.inward = jnp.where(self.has_below, self.below, self.above)
        self.outward = jnp.where(self.z == 1, self.below, self.above)
        self.order = [
            self.z,
            pick(self.z, (1, 2, 1, 2)),
            pick(self.z, (2, 0, 3, 1)),
            pick(self.z, (3, 3, 0, 0)),
        ]

    def index(self, z, x, core):
        return z * 4 + x * 2 + core


def greet(targets):
    barrier = pltpu.get_barrier_semaphore()
    for target, there in targets:
        if there is None:
            pl.semaphore_signal(barrier, inc=1, device_id={"frame": target}, device_id_type=MESH)
        else:

            @pl.when(there)
            def _():
                pl.semaphore_signal(
                    barrier, inc=1, device_id={"frame": target}, device_id_type=MESH
                )

    return barrier


STEPS = (("z", 0), ("z", 1), ("x", 0), ("z", 2), ("x", 1), ("z", 3), ("x", 2), ("x", 3))


RELAY_STEPS = (
    ("z", 0), ("z", 1), ("x", 0), ("z", 2), ("z", 3), ("x", 1), ("x", 2), ("x", 3)
)


def push(src, dst, send, recv, target):
    return pltpu.make_async_remote_copy(
        src_ref=src,
        dst_ref=dst,
        send_sem=send,
        recv_sem=recv,
        device_id={"frame": target},
        device_id_type=MESH,
    )


def piece(ref, part):
    rows = ref.shape[0] // PARTS
    return ref.at[pl.ds(part * rows, rows)]


def relays(place, k, part, src, to, send_up, send_down, send_x, arrived):
    source_z = place.order[k]
    up = jnp.logical_and(source_z <= place.z, place.has_above)
    down = jnp.logical_and(source_z >= place.z, place.has_below)
    number = k * PARTS + part
    across = None
    if k == 2:
        across = place.outer
    elif k == 3 and part == PARTS - 1:
        across = place.inner
    return [
        (push(src, to, send_x.at[number], arrived, place.across), across),
        (push(src, to, send_up.at[number], arrived, place.above), up),
        (push(src, to, send_down.at[number], arrived, place.below), down),
    ]


def crossings(place, k, part, to, send_z, arrived):
    if k == 0:
        return [(push(to, to, send_z.at[part], arrived, place.inward), place.outer)]
    if k == 3 and part == PARTS - 1:
        return [(push(to, to, send_z.at[PARTS], arrived, place.outward), place.inner)]
    return []


def start_all(copies):
    for copy, there in copies:
        if there is None:
            copy.start()
        else:
            pl.when(there)(copy.start)


def wait_sent(copies):
    for copy, there in copies:
        if there is None:
            copy.wait_send()
        else:
            pl.when(there)(copy.wait_send)


def gather_kernel(
    frames, seg, every, ids, seg1, seg8, send_up, send_down, send_x, send_z, send_core, recv,
    seg_send, seg_recv, local
):
    place = Place()
    me = place.me
    barrier = greet([(lax.rem(me + d, 16), None) for d in range(1, 16)])
    load = pltpu.make_async_copy(seg, seg1, local.at[2])
    load.start()
    load.wait()
    seg8[...] = jnp.broadcast_to(seg1[...], seg8.shape)
    own = pltpu.make_async_copy(frames, every.at[me], local.at[0])
    own.start()
    own_ids = pltpu.make_async_copy(seg8, ids.at[me], local.at[1])
    own_ids.start()
    pl.semaphore_wait(barrier, 15)
    sent = []
    for kind, k in RELAY_STEPS:
        x = place.x if kind == "z" else 1 - place.x
        slot = place.index(place.order[k], x, place.core)
        first = kind == "z" and k == 0
        for part in range(PARTS):
            to = piece(every.at[slot], part)
            src = piece(frames, part) if first else to
            arrived = recv.at[slot * PARTS + part]
            if not first:
                push(src, to, send_core.at[0], arrived, place.sibling).wait_recv()
            copies = []
            if kind == "z":
                copies = relays(place, k, part, src, to, send_up, send_down, send_x, arrived)
            else:
                copies = crossings(place, k, part, to, send_z, arrived)
            number = (k + (0 if kind == "z" else 4)) * PARTS + part
            copies.append((push(src, to, send_core.at[number], arrived, place.sibling), None))
            start_all(copies)
            sent += copies
        if first:
            for d in range(1, 16):
                copy = push(
                    seg8, ids.at[me], seg_send.at[d], seg_recv.at[d], lax.rem(me + d, 16)
                )
                copy.start()
                sent.append((copy, None))
    for kind, k in STEPS:
        x = place.x if kind == "z" else 1 - place.x
        slot = place.index(place.order[k], x, 1 - place.core)
        for part in range(PARTS):
            to = piece(every.at[slot], part)
            push(
                to, to, send_core.at[0], recv.at[slot * PARTS + part], place.sibling
            ).wait_recv()
    for d in range(1, 16):
        source = lax.rem(me - d + 16, 16)
        push(seg8, ids.at[source], seg_send.at[d], seg_recv.at[d], source).wait_recv()
    wait_sent(sent)
    own.wait()
    own_ids.wait()


def gather_frames(frames, segment):
    dma = pltpu.SemaphoreType.DMA
    rows, channels = frames.shape
    return pl.pallas_call(
        gather_kernel,
        out_shape=(
            jax.ShapeDtypeStruct((16, rows, channels), frames.dtype),
            jax.ShapeDtypeStruct((16, 8, rows), jnp.int32),
        ),
        in_specs=[pl.BlockSpec(memory_space=pl.ANY)] * 2,
        out_specs=[pl.BlockSpec(memory_space=pl.ANY)] * 2,
        scratch_shapes=[
            pltpu.VMEM((1, rows), jnp.int32),
            pltpu.VMEM((8, rows), jnp.int32),
            dma((4 * PARTS,)),
            dma((4 * PARTS,)),
            dma((4 * PARTS,)),
            dma((PARTS + 1,)),
            dma((8 * PARTS,)),
            dma((16 * PARTS,)),
            dma((16,)),
            dma((16,)),
            dma((3,)),
        ],
        compiler_params=pltpu.CompilerParams(
            collective_id=0, has_side_effects=True, vmem_limit_bytes=62 * 2**20
        ),
        name="gather_frames",
    )(frames, segment.reshape(1, rows))


def split_pair(pair):
    lane = lax.broadcasted_iota(jnp.int32, pair.shape, 1)
    zero = jnp.zeros_like(pair)
    return jnp.concatenate(
        [jnp.where(lane < HEAD_DIM, pair, zero), jnp.where(lane < HEAD_DIM, zero, pair)], axis=0
    )


def clear(peak, total, acc):
    peak[...] = jnp.full(peak.shape, -jnp.inf, jnp.float32)
    total[...] = jnp.zeros(total.shape, jnp.float32)
    acc[...] = jnp.zeros(acc.shape, jnp.float32)


def attend(pairs, queries, keys, values, peak, total, acc, keep=None):
    scores = [
        lax.dot_general(query, key, (((1,), (1,)), ((), ())), preferred_element_type=jnp.float32)
        for query, key in zip(queries, keys)
    ]
    if keep is not None:
        column = lax.broadcasted_iota(jnp.int32, scores[0].shape, 1)
        scores = [jnp.where(column < keep, score, -jnp.inf) for score in scores]
    before = [peak[p] for p in pairs]
    old_total = [total[p] for p in pairs]
    old_acc = [acc[p] for p in pairs]
    now = [
        jnp.maximum(b, jnp.max(score, axis=1, keepdims=True)) for b, score in zip(before, scores)
    ]
    half = now[0].shape[1]
    left = [jnp.exp(score[:, :half] - n) for score, n in zip(scores, now)]
    right = [jnp.exp(score[:, half:] - n) for score, n in zip(scores, now)]
    fade = [jnp.exp(b - n) for b, n in zip(before, now)]
    weights = [
        jnp.concatenate([a.astype(jnp.bfloat16), b.astype(jnp.bfloat16)], axis=1)
        for a, b in zip(left, right)
    ]
    added = [
        jnp.dot(w, value, preferred_element_type=jnp.float32) for w, value in zip(weights, values)
    ]
    new_total = [t * f + (a + b) for t, f, a, b in zip(old_total, fade, left, right)]
    new_acc = [o * f + a for o, f, a in zip(old_acc, fade, added)]
    for position, p in enumerate(pairs):
        peak[p] = now[position]
        total[p] = new_total[position]
        acc[p] = new_acc[position]


def join_pair(p, total, acc):
    rows = acc.shape[1] // 2
    result = acc[p] / jnp.sum(total[p], axis=1, keepdims=True)
    lane = lax.broadcasted_iota(jnp.int32, (rows, acc.shape[2]), 1)
    return jnp.where(lane < HEAD_DIM, result[:rows], result[rows:]).astype(jnp.bfloat16)


def pair_columns(p):
    return pl.ds(pl.multiple_of(p * 128, 128), 128)


def cross_kernel(
    ids, every, queries_all, latents_all, w_kv_all, w_out_all, mixed, normed, block, keyval, query,
    peak, total, acc, cross, queries, latents, w_kv, w_out, chosen, sems, local
):
    loads = [
        pltpu.make_async_copy(src, dst, local.at[n])
        for n, (src, dst) in enumerate(
            [(queries_all, queries), (w_kv_all, w_kv), (w_out_all, w_out), (latents_all, latents)]
        )
    ]
    for load in loads[:2]:
        load.start()
    wanted = lax.axis_index("frame") // 2 + 1
    width = queries.shape[1]
    scale = 1.0 / math.sqrt(HEAD_DIM)

    def look(r, count):
        chosen[count] = r
        return count + jnp.where(ids[r // 2, 0, lax.rem(r, 2) * 64] == wanted, 1, 0)

    count = lax.fori_loop(0, 32, look, jnp.int32(0))
    block[...] = jnp.zeros_like(block)

    def fetch(group, j):
        run = chosen[group * 4 + j]
        return pltpu.make_async_copy(
            every.at[run // 2, pl.ds(pl.multiple_of(lax.rem(run, 2) * 64, 64), 64)],
            block.at[pl.ds(j * 64, 64)],
            sems.at[j],
        )

    def fetch_all(group):
        for j in range(4):

            @pl.when(group * 4 + j < count)
            def _():
                fetch(group, j).start()

    fetch_all(0)
    for load in loads[2:]:
        load.start()
    loads[0].wait()
    for p in range(PAIRS):
        query[p] = split_pair(queries[:, p * 128 : p * 128 + 128] * scale)
    clear(peak, total, acc)
    loads[1].wait()

    @pl.loop(0, (count + 3) // 4)
    def _(group):
        for j in range(4):

            @pl.when(group * 4 + j < count)
            def _():
                fetch(group, j).wait()

        ready = layer_norm(block[...].astype(jnp.float32)).astype(jnp.bfloat16)

        @pl.loop(0, 4)
        def _(j):
            columns = pl.ds(pl.multiple_of(j * 512, 512), 512)
            keyval[:, columns] = jnp.dot(
                ready, w_kv[:, columns], preferred_element_type=jnp.float32
            ).astype(jnp.bfloat16)

        fetch_all(group + 1)
        keep = (count - group * 4) * 64

        @pl.loop(0, PAIRS // 4)
        def _(group):
            pairs = [group * 4 + i for i in range(4)]
            attend(
                pairs,
                [query[p] for p in pairs],
                [keyval[:, pair_columns(p)] for p in pairs],
                [keyval[:, pair_columns(p + PAIRS)] for p in pairs],
                peak,
                total,
                acc,
                keep,
            )

    for p in range(PAIRS):
        cross[:, p * 128 : p * 128 + 128] = join_pair(p, total, acc)
    loads[2].wait()
    loads[3].wait()
    whole = latents[...].astype(jnp.float32) + jnp.dot(
        cross[...], w_out[...], preferred_element_type=jnp.float32
    )
    mixed[...] = whole
    normed[...] = layer_norm(whole).astype(jnp.bfloat16)


def cross_attend(ids, every, queries, latents, w_kv, w_out):
    rows, width = latents.shape
    vmem = pl.BlockSpec(memory_space=pltpu.VMEM)
    return pl.pallas_call(
        cross_kernel,
        out_shape=(
            jax.ShapeDtypeStruct((rows, width), jnp.float32),
            jax.ShapeDtypeStruct((rows, width), jnp.bfloat16),
        ),
        in_specs=[
            pl.BlockSpec(memory_space=pltpu.SMEM),
            *[pl.BlockSpec(memory_space=pl.ANY)] * 5,
        ],
        out_specs=[vmem, vmem],
        scratch_shapes=[
            pltpu.VMEM((256, every.shape[2]), jnp.bfloat16),
            pltpu.VMEM((256, 2 * width), jnp.bfloat16),
            pltpu.VMEM((PAIRS, 2 * rows, 128), jnp.bfloat16),
            pltpu.VMEM((PAIRS, 2 * rows, 128), jnp.float32),
            pltpu.VMEM((PAIRS, 2 * rows, 128), jnp.float32),
            pltpu.VMEM((PAIRS, 2 * rows, 128), jnp.float32),
            pltpu.VMEM((rows, width), jnp.bfloat16),
            pltpu.VMEM(queries.shape, jnp.bfloat16),
            pltpu.VMEM(latents.shape, jnp.bfloat16),
            pltpu.VMEM(w_kv.shape, jnp.bfloat16),
            pltpu.VMEM(w_out.shape, jnp.bfloat16),
            pltpu.SMEM((64,), jnp.int32),
            pltpu.SemaphoreType.DMA((4,)),
            pltpu.SemaphoreType.DMA((4,)),
        ],
        compiler_params=pltpu.CompilerParams(vmem_limit_bytes=56 * 2**20),
        name="cross_attend",
    )(ids, every, queries, latents, w_kv, w_out)


def self_kernel(
    normed, mixed, w_qkv, w_out, out, gathered, keyval, weights, weights_out, query, peak, total,
    acc, joined, send_up, send_down, send_x, send_z, send_core, recv, recv_core, local
):
    place = Place()
    me = place.me
    rows, width = normed.shape
    scale = 1.0 / math.sqrt(HEAD_DIM)
    barrier = greet(
        [
            (place.sibling, None),
            (place.across, None),
            (place.above, place.has_above),
            (place.below, place.has_below),
        ]
    )
    load = pltpu.make_async_copy(w_qkv, weights, local.at[0])
    load.start()
    load_out = pltpu.make_async_copy(w_out, weights_out, local.at[1])
    load_out.start()
    pl.semaphore_wait(
        barrier,
        2 + jnp.where(place.has_above, 1, 0) + jnp.where(place.has_below, 1, 0),
    )
    clear(peak, total, acc)
    sent = []

    def hand_on(k, when=None):
        slot = place.index(place.order[k], place.x, place.core)
        pieces = []
        for part in range(PARTS):
            to = piece(gathered.at[slot], part)
            src = piece(normed, part) if k == 0 else to
            arrived = recv.at[slot * PARTS + part]
            copies = relays(place, k, part, src, to, send_up, send_down, send_x, arrived)
            landing = push(src, to, send_x.at[0], arrived, place.across) if k > 0 else None
            pieces.append((landing, copies))

        def go():
            for landing, copies in pieces:
                if landing is not None:
                    landing.wait_recv()
                start_all(copies)

        if when is None:
            go()
        else:
            pl.when(when)(go)
        return [copy for _, copies in pieces for copy in copies]

    def hand_across(k, when):
        slot = place.index(place.order[k], 1 - place.x, place.core)
        pieces = []
        for part in range(PARTS):
            to = piece(gathered.at[slot], part)
            arrived = recv.at[slot * PARTS + part]
            landing = push(to, to, send_x.at[0], arrived, place.across)
            pieces.append((landing, crossings(place, k, part, to, send_z, arrived)))

        @pl.when(when)
        def _():
            for landing, copies in pieces:
                landing.wait_recv()
                for copy, _ in copies:
                    copy.start()

        return [copy for _, copies in pieces for copy in copies]

    def take(step):
        kind, k = STEPS[step]
        x = place.x if kind == "z" else 1 - place.x
        slot = place.index(place.order[k], x, place.core)
        chip = place.order[k] * 2 + x
        src = normed if step == 0 else gathered.at[slot]
        if kind == "x":
            landings = []
            for part in range(PARTS):
                to = piece(gathered.at[slot], part)
                arrived = recv.at[slot * PARTS + part]
                landings.append(push(to, to, send_x.at[0], arrived, place.across))

            def land():
                for landing in landings:
                    landing.wait_recv()

            if k == 0:
                pl.when(place.inner)(land)
            elif k == 3:
                pl.when(place.outer)(land)
            else:
                land()
        if step == 0:
            load.wait()

            @pl.loop(0, PAIRS // 2)
            def _(j):
                columns = pl.ds(pl.multiple_of(j * 256, 256), 256)
                part = jnp.dot(normed[...], weights[:, columns], preferred_element_type=jnp.float32)
                part = part.astype(jnp.bfloat16) * scale
                query[2 * j] = split_pair(part[:, :128])
                query[2 * j + 1] = split_pair(part[:, 128:])

        @pl.loop(0, 4)
        def _(j):
            columns = pl.ds(pl.multiple_of(j * 512, 512), 512)
            wide = pl.ds(pl.multiple_of(width + j * 512, 512), 512)
            keyval[chip, place.core, :, columns] = jnp.dot(
                src[...], weights[:, wide], preferred_element_type=jnp.float32
            ).astype(jnp.bfloat16)

        ours = keyval.at[chip, place.core]
        copy = push(ours, ours, send_core.at[step], recv_core.at[step], place.sibling)
        copy.start()
        sent.append((copy, None))
        return chip

    def use(step, chip):
        theirs = keyval.at[chip, 1 - place.core]
        push(theirs, theirs, send_core.at[step], recv_core.at[step], place.sibling).wait_recv()

        @pl.loop(0, PAIRS // 4)
        def _(group):
            pairs = [group * 4 + i for i in range(4)]
            attend(
                pairs,
                [query[p] for p in pairs],
                [keyval[chip, :, :, pair_columns(p)].reshape(2 * rows, 128) for p in pairs],
                [
                    keyval[chip, :, :, pair_columns(p + PAIRS)].reshape(2 * rows, 128)
                    for p in pairs
                ],
                peak,
                total,
                acc,
            )

    sent += hand_on(0)
    chip = take(0)
    for step in range(1, len(STEPS)):
        if step == 1:
            sent += hand_on(1)
            sent += hand_across(0, place.outer)
            sent += hand_on(2, place.inner)
        elif step == 3:
            hand_on(2, place.outer)
            sent += hand_on(3, place.inner)
        elif step == 5:
            hand_on(3, place.outer)
        elif step == 6:
            sent += hand_across(3, place.inner)
        later = take(step)
        use(step - 1, chip)
        chip = later
    use(len(STEPS) - 1, chip)
    for p in range(PAIRS):
        joined[:, p * 128 : p * 128 + 128] = join_pair(p, total, acc)
    load_out.wait()
    out[...] = (
        mixed[...] + jnp.dot(joined[...], weights_out[...], preferred_element_type=jnp.float32)
    ).astype(jnp.bfloat16)
    wait_sent(sent)


def self_attend(normed, mixed, w_qkv, w_out):
    rows, width = normed.shape
    dma = pltpu.SemaphoreType.DMA
    vmem = pl.BlockSpec(memory_space=pltpu.VMEM)
    anywhere = pl.BlockSpec(memory_space=pl.ANY)
    return pl.pallas_call(
        self_kernel,
        out_shape=jax.ShapeDtypeStruct((rows, width), jnp.bfloat16),
        in_specs=[vmem, vmem, anywhere, anywhere],
        out_specs=vmem,
        scratch_shapes=[
            pltpu.VMEM((16, rows, width), jnp.bfloat16),
            pltpu.VMEM((8, 2, rows, 2 * width), jnp.bfloat16),
            pltpu.VMEM(w_qkv.shape, jnp.bfloat16),
            pltpu.VMEM(w_out.shape, jnp.bfloat16),
            pltpu.VMEM((PAIRS, 2 * rows, 128), jnp.bfloat16),
            pltpu.VMEM((PAIRS, 2 * rows, 128), jnp.float32),
            pltpu.VMEM((PAIRS, 2 * rows, 128), jnp.float32),
            pltpu.VMEM((PAIRS, 2 * rows, 128), jnp.float32),
            pltpu.VMEM((rows, width), jnp.bfloat16),
            dma((4 * PARTS,)),
            dma((4 * PARTS,)),
            dma((4 * PARTS,)),
            dma((PARTS + 1,)),
            dma((8,)),
            dma((16 * PARTS,)),
            dma((8,)),
            dma((2,)),
        ],
        compiler_params=pltpu.CompilerParams(
            collective_id=1, has_side_effects=True, vmem_limit_bytes=57 * 2**20
        ),
        name="self_attend",
    )(normed, mixed, w_qkv, w_out)


def shards_small(frames, segment, latents, latent_queries, w_kv, w_cross_out, w_self_qkv, w_self_out):
    every, ids = gather_frames(frames, segment)
    mixed, normed = cross_attend(ids, every, latent_queries, latents, w_kv, w_cross_out)
    return self_attend(normed, mixed, w_self_qkv, w_self_out)


def solution(mesh):
    placed = (
        P(("rep", "frame"), None),
        P(("rep", "frame")),
        P("frame", None),
        P("frame", None),
        P(),
        P(),
        P(),
        P(),
    )
    body = shards_small if mesh.shape["frame"] == 2 * NX * NZ else shards
    return jax.shard_map(
        body, mesh=mesh, in_specs=placed, out_specs=P(("rep", "frame"), None), check_vma=False
    )
```

```python
import math

import jax
import jax.numpy as jnp
from jax import lax
from jax.experimental import pallas as pl
from jax.experimental.pallas import tpu as pltpu
from jax.sharding import PartitionSpec as P

H = 16
HEAD_DIM = 64
L = 2048
NB = 8


NEG = -1e30


def layer_norm(inputs):
    centre = inputs - jnp.mean(inputs, axis=-1, keepdims=True)
    spread = jnp.mean(centre * centre, axis=-1, keepdims=True)
    return centre * lax.rsqrt(spread + 1e-05)


def shards(frames, segment, latents, latent_queries, w_kv, w_cross_out, w_self_qkv, w_self_out):
    feature_width = w_kv.shape[1] // 2
    owned_rows = latents.shape[0]
    frame_count = frames.shape[0]
    scale = 1.0 / math.sqrt(HEAD_DIM)
    block_rows = L // NB
    latent_full = latents.astype(jnp.float32)
    normed = layer_norm(frames.astype(jnp.float32)).astype(jnp.bfloat16)
    keyval = jnp.dot(normed, w_kv, preferred_element_type=jnp.float32).astype(jnp.bfloat16)
    key_heads = keyval[:, :feature_width].reshape(frame_count, H, HEAD_DIM).transpose(1, 0, 2)
    value_heads = keyval[:, feature_width:].reshape(frame_count, H, HEAD_DIM).transpose(1, 0, 2)
    total_rows = owned_rows * lax.axis_size("frame")
    piece = lax.all_gather(latent_queries, "frame", axis=0, tiled=True)
    piece_rows = piece.shape[0]
    block_ids = jnp.arange(piece_rows, dtype=jnp.int32) // block_rows + 1
    allowed = segment[None, :] == block_ids[:, None]
    query_heads = piece.reshape(piece_rows, H, HEAD_DIM).transpose(1, 0, 2)

    def one_head(item):
        query_head, key_head, value_head = item
        score = (
            jnp.einsum("re,fe->rf", query_head, key_head, preferred_element_type=jnp.float32)
            * scale
        )
        score = jnp.where(allowed, score, NEG)
        block_max = jnp.max(score, axis=1)
        weights = jnp.where(allowed, jnp.exp(score - block_max[:, None]), 0.0)
        block_total = jnp.sum(weights, axis=1)
        summed = jnp.dot(
            weights.astype(jnp.bfloat16), value_head, preferred_element_type=jnp.float32
        )
        return (block_max, block_total, summed)

    block_max, block_total, summed = lax.map(one_head, (query_heads, key_heads, value_heads))
    run_max = block_max.T
    run_total = block_total.T
    joined = summed.transpose(1, 0, 2).reshape(piece_rows, feature_width)
    run_acc = joined
    run_max, run_total, run_acc = (run_max, run_total, run_acc)
    sources = lax.axis_size("frame")
    got_acc, got_max, got_total = (
        lax.all_to_all(
            run_acc.reshape(sources, owned_rows, feature_width),
            "frame",
            split_axis=0,
            concat_axis=0,
            tiled=True,
        ),
        lax.all_to_all(
            run_max.reshape(sources, owned_rows, H),
            "frame",
            split_axis=0,
            concat_axis=0,
            tiled=True,
        ),
        lax.all_to_all(
            run_total.reshape(sources, owned_rows, H),
            "frame",
            split_axis=0,
            concat_axis=0,
            tiled=True,
        ),
    )
    global_max = jnp.max(got_max, axis=0)
    factor = jnp.exp(got_max - global_max[None])
    norms = jnp.sum(got_total * factor, axis=0)
    sums = jnp.sum(
        got_acc.reshape(sources, owned_rows, H, HEAD_DIM) * factor[:, :, :, None], axis=0
    )
    cross = (sums / norms[:, :, None]).reshape(owned_rows, feature_width)
    cross = cross.astype(jnp.bfloat16)
    mixed = latent_full + jnp.dot(cross, w_cross_out, preferred_element_type=jnp.float32)
    normed_latent = layer_norm(mixed).astype(jnp.bfloat16)
    triple = jnp.dot(normed_latent, w_self_qkv, preferred_element_type=jnp.float32).astype(
        jnp.bfloat16
    )
    self_query = triple[:, :feature_width].reshape(owned_rows, H, HEAD_DIM)
    self_key = triple[:, feature_width : 2 * feature_width]
    self_value = triple[:, 2 * feature_width :]
    every_key, every_value = (
        lax.all_gather(self_key, "frame", axis=0, tiled=True),
        lax.all_gather(self_value, "frame", axis=0, tiled=True),
    )
    every_key = every_key.reshape(total_rows, H, HEAD_DIM)
    every_value = every_value.reshape(total_rows, H, HEAD_DIM)
    score = (
        jnp.einsum("rhe,mhe->hrm", self_query, every_key, preferred_element_type=jnp.float32)
        * scale
    )
    peak = jnp.max(score, axis=2, keepdims=True)
    expo = jnp.exp(score - peak)
    probs = (expo / jnp.sum(expo, axis=2, keepdims=True)).astype(jnp.bfloat16)
    attended = jnp.einsum("hrm,mhe->rhe", probs, every_value, preferred_element_type=jnp.float32)
    attended = attended.reshape(owned_rows, feature_width).astype(jnp.bfloat16)
    return (mixed + jnp.dot(attended, w_self_out, preferred_element_type=jnp.float32)).astype(
        jnp.bfloat16
    )


PARTS = 2
NX = 2
NZ = 4
PAIRS = H // 2
MESH = pl.DeviceIdType.MESH


def pick(index, values):
    chosen = values[0]
    for position in range(1, len(values)):
        chosen = jnp.where(index == position, values[position], chosen)
    return chosen


class Place:
    def __init__(self):
        self.me = lax.axis_index("frame")
        self.z = self.me // 4
        self.x = lax.rem(self.me // 2, 2)
        self.core = lax.rem(self.me, 2)
        self.sibling = self.index(self.z, self.x, 1 - self.core)
        self.across = self.index(self.z, 1 - self.x, self.core)
        self.above = self.me + 4
        self.below = self.me - 4
        self.has_above = self.z < NZ - 1
        self.has_below = self.z > 0
        self.order = [
            self.z,
            pick(self.z, (1, 2, 1, 2)),
            pick(self.z, (2, 0, 3, 1)),
            pick(self.z, (3, 3, 0, 0)),
        ]

    def index(self, z, x, core):
        return z * 4 + x * 2 + core


def greet(targets):
    barrier = pltpu.get_barrier_semaphore()
    for target, there in targets:
        if there is None:
            pl.semaphore_signal(barrier, inc=1, device_id={"frame": target}, device_id_type=MESH)
        else:

            @pl.when(there)
            def _():
                pl.semaphore_signal(
                    barrier, inc=1, device_id={"frame": target}, device_id_type=MESH
                )

    return barrier


STEPS = (("z", 0), ("z", 1), ("x", 0), ("z", 2), ("x", 1), ("z", 3), ("x", 2), ("x", 3))


def push(src, dst, send, recv, target):
    return pltpu.make_async_remote_copy(
        src_ref=src,
        dst_ref=dst,
        send_sem=send,
        recv_sem=recv,
        device_id={"frame": target},
        device_id_type=MESH,
    )


def piece(ref, part):
    rows = ref.shape[0] // PARTS
    return ref.at[pl.ds(part * rows, rows)]


def relays(place, k, part, src, to, send_up, send_down, send_x, arrived):
    source_z = place.order[k]
    up = jnp.logical_and(source_z <= place.z, place.has_above)
    down = jnp.logical_and(source_z >= place.z, place.has_below)
    number = k * PARTS + part
    return [
        (push(src, to, send_x.at[number], arrived, place.across), None),
        (push(src, to, send_up.at[number], arrived, place.above), up),
        (push(src, to, send_down.at[number], arrived, place.below), down),
    ]


def start_all(copies):
    for copy, there in copies:
        if there is None:
            copy.start()
        else:
            pl.when(there)(copy.start)


def wait_sent(copies):
    for copy, there in copies:
        if there is None:
            copy.wait_send()
        else:
            pl.when(there)(copy.wait_send)


def gather_kernel(
    frames, seg, every, ids, seg1, seg8, send_up, send_down, send_x, send_core, recv, seg_send,
    seg_recv, local
):
    place = Place()
    me = place.me
    barrier = greet([(lax.rem(me + d, 16), None) for d in range(1, 16)])
    load = pltpu.make_async_copy(seg, seg1, local.at[2])
    load.start()
    load.wait()
    seg8[...] = jnp.broadcast_to(seg1[...], seg8.shape)
    own = pltpu.make_async_copy(frames, every.at[me], local.at[0])
    own.start()
    own_ids = pltpu.make_async_copy(seg8, ids.at[me], local.at[1])
    own_ids.start()
    pl.semaphore_wait(barrier, 15)
    sent = []
    for kind, k in [("z", 0), ("z", 1), ("z", 2), ("z", 3), ("x", 0), ("x", 1), ("x", 2), ("x", 3)]:
        x = place.x if kind == "z" else 1 - place.x
        slot = place.index(place.order[k], x, place.core)
        first = kind == "z" and k == 0
        for part in range(PARTS):
            to = piece(every.at[slot], part)
            src = piece(frames, part) if first else to
            arrived = recv.at[slot * PARTS + part]
            if not first:
                push(src, to, send_core.at[0], arrived, place.sibling).wait_recv()
            copies = []
            if kind == "z":
                copies = relays(place, k, part, src, to, send_up, send_down, send_x, arrived)
            number = (k + (0 if kind == "z" else 4)) * PARTS + part
            copies.append((push(src, to, send_core.at[number], arrived, place.sibling), None))
            start_all(copies)
            sent += copies
        if first:
            for d in range(1, 16):
                copy = push(
                    seg8, ids.at[me], seg_send.at[d], seg_recv.at[d], lax.rem(me + d, 16)
                )
                copy.start()
                sent.append((copy, None))
    for kind, k in STEPS:
        x = place.x if kind == "z" else 1 - place.x
        slot = place.index(place.order[k], x, 1 - place.core)
        for part in range(PARTS):
            to = piece(every.at[slot], part)
            push(
                to, to, send_core.at[0], recv.at[slot * PARTS + part], place.sibling
            ).wait_recv()
    for d in range(1, 16):
        source = lax.rem(me - d + 16, 16)
        push(seg8, ids.at[source], seg_send.at[d], seg_recv.at[d], source).wait_recv()
    wait_sent(sent)
    own.wait()
    own_ids.wait()


def gather_frames(frames, segment):
    dma = pltpu.SemaphoreType.DMA
    rows, channels = frames.shape
    return pl.pallas_call(
        gather_kernel,
        out_shape=(
            jax.ShapeDtypeStruct((16, rows, channels), frames.dtype),
            jax.ShapeDtypeStruct((16, 8, rows), jnp.int32),
        ),
        in_specs=[pl.BlockSpec(memory_space=pl.ANY)] * 2,
        out_specs=[pl.BlockSpec(memory_space=pl.ANY)] * 2,
        scratch_shapes=[
            pltpu.VMEM((1, rows), jnp.int32),
            pltpu.VMEM((8, rows), jnp.int32),
            dma((4 * PARTS,)),
            dma((4 * PARTS,)),
            dma((4 * PARTS,)),
            dma((8 * PARTS,)),
            dma((16 * PARTS,)),
            dma((16,)),
            dma((16,)),
            dma((3,)),
        ],
        compiler_params=pltpu.CompilerParams(
            collective_id=0, has_side_effects=True, vmem_limit_bytes=62 * 2**20
        ),
        name="gather_frames",
    )(frames, segment.reshape(1, rows))


LOADS = 8


class Load:
    def __init__(self, src, dst, sems):
        rows = src.shape[0] // LOADS
        shares = [pl.ds(n * rows, rows) for n in range(LOADS)]
        self.copies = [
            pltpu.make_async_copy(src.at[share], dst.at[share], sems.at[n])
            for n, share in enumerate(shares)
        ]

    def start(self):
        for copy in self.copies:
            copy.start()

    def wait(self):
        for copy in self.copies:
            copy.wait()


def split_pair(pair):
    lane = lax.broadcasted_iota(jnp.int32, pair.shape, 1)
    zero = jnp.zeros_like(pair)
    return jnp.concatenate(
        [jnp.where(lane < HEAD_DIM, pair, zero), jnp.where(lane < HEAD_DIM, zero, pair)], axis=0
    )


def clear(peak, total, acc):
    peak[...] = jnp.full(peak.shape, -jnp.inf, jnp.float32)
    total[...] = jnp.zeros(total.shape, jnp.float32)
    acc[...] = jnp.zeros(acc.shape, jnp.float32)


def attend(pairs, queries, keys, values, peak, total, acc, keep=None):
    scores = [
        lax.dot_general(query, key, (((1,), (1,)), ((), ())), preferred_element_type=jnp.float32)
        for query, key in zip(queries, keys)
    ]
    if keep is not None:
        column = lax.broadcasted_iota(jnp.int32, scores[0].shape, 1)
        scores = [jnp.where(column < keep, score, -jnp.inf) for score in scores]
    before = [peak[p] for p in pairs]
    old_total = [total[p] for p in pairs]
    old_acc = [acc[p] for p in pairs]
    now = [
        jnp.maximum(b, jnp.max(score, axis=1, keepdims=True)) for b, score in zip(before, scores)
    ]
    half = now[0].shape[1]
    left = [jnp.exp(score[:, :half] - n) for score, n in zip(scores, now)]
    right = [jnp.exp(score[:, half:] - n) for score, n in zip(scores, now)]
    fade = [jnp.exp(b - n) for b, n in zip(before, now)]
    weights = [
        jnp.concatenate([a.astype(jnp.bfloat16), b.astype(jnp.bfloat16)], axis=1)
        for a, b in zip(left, right)
    ]
    added = [
        jnp.dot(w, value, preferred_element_type=jnp.float32) for w, value in zip(weights, values)
    ]
    new_total = [t * f + (a + b) for t, f, a, b in zip(old_total, fade, left, right)]
    new_acc = [o * f + a for o, f, a in zip(old_acc, fade, added)]
    for position, p in enumerate(pairs):
        peak[p] = now[position]
        total[p] = new_total[position]
        acc[p] = new_acc[position]


def join_pair(p, total, acc):
    rows = acc.shape[1] // 2
    result = acc[p] / jnp.sum(total[p], axis=1, keepdims=True)
    lane = lax.broadcasted_iota(jnp.int32, (rows, acc.shape[2]), 1)
    return jnp.where(lane < HEAD_DIM, result[:rows], result[rows:]).astype(jnp.bfloat16)


def pair_columns(p):
    return pl.ds(pl.multiple_of(p * 128, 128), 128)


def cross_kernel(
    ids, every, queries_all, latents_all, w_kv_all, w_out_all, mixed, normed, block, keyval, query,
    peak, total, acc, cross, queries, latents, w_kv, w_out, chosen, sems, local
):
    loads = [
        Load(src, dst, local.at[n])
        for n, (src, dst) in enumerate(
            [(queries_all, queries), (w_kv_all, w_kv), (w_out_all, w_out), (latents_all, latents)]
        )
    ]
    for load in loads[:2]:
        load.start()
    wanted = lax.axis_index("frame") // 2 + 1
    width = queries.shape[1]
    scale = 1.0 / math.sqrt(HEAD_DIM)

    def look(r, count):
        chosen[count] = r
        return count + jnp.where(ids[r // 2, 0, lax.rem(r, 2) * 64] == wanted, 1, 0)

    count = lax.fori_loop(0, 32, look, jnp.int32(0))
    block[...] = jnp.zeros_like(block)

    def fetch(group, j):
        run = chosen[group * 4 + j]
        return pltpu.make_async_copy(
            every.at[run // 2, pl.ds(pl.multiple_of(lax.rem(run, 2) * 64, 64), 64)],
            block.at[pl.ds(j * 64, 64)],
            sems.at[j],
        )

    def fetch_all(group):
        for j in range(4):

            @pl.when(group * 4 + j < count)
            def _():
                fetch(group, j).start()

    fetch_all(0)
    for load in loads[2:]:
        load.start()
    loads[0].wait()
    for p in range(PAIRS):
        query[p] = split_pair(queries[:, p * 128 : p * 128 + 128] * scale)
    clear(peak, total, acc)
    loads[1].wait()

    @pl.loop(0, (count + 3) // 4)
    def _(group):
        for j in range(4):

            @pl.when(group * 4 + j < count)
            def _():
                fetch(group, j).wait()

        ready = layer_norm(block[...].astype(jnp.float32)).astype(jnp.bfloat16)

        @pl.loop(0, 4)
        def _(j):
            columns = pl.ds(pl.multiple_of(j * 512, 512), 512)
            keyval[:, columns] = jnp.dot(
                ready, w_kv[:, columns], preferred_element_type=jnp.float32
            ).astype(jnp.bfloat16)

        fetch_all(group + 1)
        keep = (count - group * 4) * 64

        @pl.loop(0, PAIRS // 4)
        def _(group):
            pairs = [group * 4 + i for i in range(4)]
            attend(
                pairs,
                [query[p] for p in pairs],
                [keyval[:, pair_columns(p)] for p in pairs],
                [keyval[:, pair_columns(p + PAIRS)] for p in pairs],
                peak,
                total,
                acc,
                keep,
            )

    for p in range(PAIRS):
        cross[:, p * 128 : p * 128 + 128] = join_pair(p, total, acc)
    loads[2].wait()
    loads[3].wait()
    whole = latents[...].astype(jnp.float32) + jnp.dot(
        cross[...], w_out[...], preferred_element_type=jnp.float32
    )
    mixed[...] = whole
    normed[...] = layer_norm(whole).astype(jnp.bfloat16)


def cross_attend(ids, every, queries, latents, w_kv, w_out):
    rows, width = latents.shape
    vmem = pl.BlockSpec(memory_space=pltpu.VMEM)
    return pl.pallas_call(
        cross_kernel,
        out_shape=(
            jax.ShapeDtypeStruct((rows, width), jnp.float32),
            jax.ShapeDtypeStruct((rows, width), jnp.bfloat16),
        ),
        in_specs=[
            pl.BlockSpec(memory_space=pltpu.SMEM),
            *[pl.BlockSpec(memory_space=pl.ANY)] * 5,
        ],
        out_specs=[vmem, vmem],
        scratch_shapes=[
            pltpu.VMEM((256, every.shape[2]), jnp.bfloat16),
            pltpu.VMEM((256, 2 * width), jnp.bfloat16),
            pltpu.VMEM((PAIRS, 2 * rows, 128), jnp.bfloat16),
            pltpu.VMEM((PAIRS, 2 * rows, 128), jnp.float32),
            pltpu.VMEM((PAIRS, 2 * rows, 128), jnp.float32),
            pltpu.VMEM((PAIRS, 2 * rows, 128), jnp.float32),
            pltpu.VMEM((rows, width), jnp.bfloat16),
            pltpu.VMEM(queries.shape, jnp.bfloat16),
            pltpu.VMEM(latents.shape, jnp.bfloat16),
            pltpu.VMEM(w_kv.shape, jnp.bfloat16),
            pltpu.VMEM(w_out.shape, jnp.bfloat16),
            pltpu.SMEM((64,), jnp.int32),
            pltpu.SemaphoreType.DMA((4,)),
            pltpu.SemaphoreType.DMA((4, LOADS)),
        ],
        compiler_params=pltpu.CompilerParams(vmem_limit_bytes=61 * 2**20),
        name="cross_attend",
    )(ids, every, queries, latents, w_kv, w_out)


def self_kernel(
    normed, mixed, w_qkv, w_out, out, gathered, keyval, weights, weights_out, query, peak, total,
    acc, joined, send_up, send_down, send_x, send_core, recv, recv_core, local
):
    place = Place()
    me = place.me
    rows, width = normed.shape
    scale = 1.0 / math.sqrt(HEAD_DIM)
    barrier = greet(
        [
            (place.sibling, None),
            (place.across, None),
            (place.above, place.has_above),
            (place.below, place.has_below),
        ]
    )
    load = Load(w_qkv, weights, local.at[0])
    load.start()
    load_out = Load(w_out, weights_out, local.at[1])
    load_out.start()
    pl.semaphore_wait(
        barrier,
        2 + jnp.where(place.has_above, 1, 0) + jnp.where(place.has_below, 1, 0),
    )
    clear(peak, total, acc)
    sent = []

    def hand_on(k, when=None):
        slot = place.index(place.order[k], place.x, place.core)
        pieces = []
        for part in range(PARTS):
            to = piece(gathered.at[slot], part)
            src = piece(normed, part) if k == 0 else to
            arrived = recv.at[slot * PARTS + part]
            copies = relays(place, k, part, src, to, send_up, send_down, send_x, arrived)
            landing = push(src, to, send_x.at[0], arrived, place.across) if k > 0 else None
            pieces.append((landing, copies))

        def go():
            for landing, copies in pieces:
                if landing is not None:
                    landing.wait_recv()
                start_all(copies)

        if when is None:
            go()
        else:
            pl.when(when)(go)
        return [copy for _, copies in pieces for copy in copies]

    def take(step):
        kind, k = STEPS[step]
        x = place.x if kind == "z" else 1 - place.x
        slot = place.index(place.order[k], x, place.core)
        chip = place.order[k] * 2 + x
        src = normed if step == 0 else gathered.at[slot]
        if kind == "x":
            for part in range(PARTS):
                to = piece(gathered.at[slot], part)
                arrived = recv.at[slot * PARTS + part]
                push(to, to, send_x.at[0], arrived, place.across).wait_recv()
        if step == 0:
            load.wait()

            @pl.loop(0, PAIRS // 2)
            def _(j):
                columns = pl.ds(pl.multiple_of(j * 256, 256), 256)
                part = jnp.dot(normed[...], weights[:, columns], preferred_element_type=jnp.float32)
                part = part.astype(jnp.bfloat16) * scale
                query[2 * j] = split_pair(part[:, :128])
                query[2 * j + 1] = split_pair(part[:, 128:])

        @pl.loop(0, 4)
        def _(j):
            columns = pl.ds(pl.multiple_of(j * 512, 512), 512)
            wide = pl.ds(pl.multiple_of(width + j * 512, 512), 512)
            keyval[chip, place.core, :, columns] = jnp.dot(
                src[...], weights[:, wide], preferred_element_type=jnp.float32
            ).astype(jnp.bfloat16)

        ours = keyval.at[chip, place.core]
        copy = push(ours, ours, send_core.at[step], recv_core.at[step], place.sibling)
        copy.start()
        sent.append((copy, None))
        return chip

    def use(step, chip):
        theirs = keyval.at[chip, 1 - place.core]
        push(theirs, theirs, send_core.at[step], recv_core.at[step], place.sibling).wait_recv()

        @pl.loop(0, PAIRS // 4)
        def _(group):
            pairs = [group * 4 + i for i in range(4)]
            attend(
                pairs,
                [query[p] for p in pairs],
                [keyval[chip, :, :, pair_columns(p)].reshape(2 * rows, 128) for p in pairs],
                [
                    keyval[chip, :, :, pair_columns(p + PAIRS)].reshape(2 * rows, 128)
                    for p in pairs
                ],
                peak,
                total,
                acc,
            )

    inner = jnp.logical_and(place.has_above, place.has_below)
    outer = jnp.logical_not(inner)
    sent += hand_on(0)
    chip = take(0)
    for step in range(1, len(STEPS)):
        if step == 1:
            sent += hand_on(1)
            sent += hand_on(2, inner)
        elif step == 3:
            hand_on(2, outer)
            sent += hand_on(3, inner)
        elif step == 5:
            hand_on(3, outer)
        later = take(step)
        use(step - 1, chip)
        chip = later
    use(len(STEPS) - 1, chip)
    for p in range(PAIRS):
        joined[:, p * 128 : p * 128 + 128] = join_pair(p, total, acc)
    load_out.wait()
    out[...] = (
        mixed[...] + jnp.dot(joined[...], weights_out[...], preferred_element_type=jnp.float32)
    ).astype(jnp.bfloat16)
    wait_sent(sent)


def self_attend(normed, mixed, w_qkv, w_out):
    rows, width = normed.shape
    dma = pltpu.SemaphoreType.DMA
    vmem = pl.BlockSpec(memory_space=pltpu.VMEM)
    anywhere = pl.BlockSpec(memory_space=pl.ANY)
    return pl.pallas_call(
        self_kernel,
        out_shape=jax.ShapeDtypeStruct((rows, width), jnp.bfloat16),
        in_specs=[vmem, vmem, anywhere, anywhere],
        out_specs=vmem,
        scratch_shapes=[
            pltpu.VMEM((16, rows, width), jnp.bfloat16),
            pltpu.VMEM((8, 2, rows, 2 * width), jnp.bfloat16),
            pltpu.VMEM(w_qkv.shape, jnp.bfloat16),
            pltpu.VMEM(w_out.shape, jnp.bfloat16),
            pltpu.VMEM((PAIRS, 2 * rows, 128), jnp.bfloat16),
            pltpu.VMEM((PAIRS, 2 * rows, 128), jnp.float32),
            pltpu.VMEM((PAIRS, 2 * rows, 128), jnp.float32),
            pltpu.VMEM((PAIRS, 2 * rows, 128), jnp.float32),
            pltpu.VMEM((rows, width), jnp.bfloat16),
            dma((4 * PARTS,)),
            dma((4 * PARTS,)),
            dma((4 * PARTS,)),
            dma((8,)),
            dma((16 * PARTS,)),
            dma((8,)),
            dma((2, LOADS)),
        ],
        compiler_params=pltpu.CompilerParams(
            collective_id=1, has_side_effects=True, vmem_limit_bytes=60 * 2**20
        ),
        name="self_attend",
    )(normed, mixed, w_qkv, w_out)


def shards_small(frames, segment, latents, latent_queries, w_kv, w_cross_out, w_self_qkv, w_self_out):
    every, ids = gather_frames(frames, segment)
    mixed, normed = cross_attend(ids, every, latent_queries, latents, w_kv, w_cross_out)
    return self_attend(normed, mixed, w_self_qkv, w_self_out)


def solution(mesh):
    placed = (
        P(("rep", "frame"), None),
        P(("rep", "frame")),
        P("frame", None),
        P("frame", None),
        P(),
        P(),
        P(),
        P(),
    )
    body = shards_small if mesh.shape["frame"] == 2 * NX * NZ else shards
    return jax.shard_map(
        body, mesh=mesh, in_specs=placed, out_specs=P(("rep", "frame"), None), check_vma=False
    )
```
